128 devices in a mesh: wave: 4 (over z), tile: 32 (over y, x, core).
Axes of the slice: x: 4, y: 4, z: 4, core: 2. Of those that a mesh axis runs over, the one named last changes fastest.
Arguments:
- initial_fields: bfloat16 [16, 8, 1024, 1024], P('wave', None, 'tile'), may hold values from -6 to 6
- conductivity: float32 [1024, 1024], P('tile'), may hold values from 0.1 to 10
- wavenumbers: float32 [16], replicated, may hold values from 0.05 to 1.5
- quad_weights: float32 [16], replicated, may hold values from 0.05 to 0.3
- sweep_counts: int32 [16], replicated, may hold values from 1 to 8, as said below
- electrode_cells: int32 [64], replicated, may hold values from 0 to 1023
- source_pairs: int32 [8, 2], replicated, may hold values from 0 to 63, as said below
Outputs:
- potential: float32 [8, 1024, 1024], P('wave', 'tile')
The draws below stay inside these ranges and needn't reach their ends.
Inputs may be any that keep to these rules, and one draw needn't show every extreme that they name: `sweep_counts`: each wavenumber gets at least one sweep and at most 8. `source_pairs`: the two electrodes of a source column are different electrodes.
All inputs are finite; a program needn't handle non-finite values.
Results may differ from the reference program's by a relative error of at most 0.0003.
Values may be sent and summed in bfloat16 or wider, within the bound.
A program may use at most 64 MiB of HBM per device.

```python
import math
import jax
import jax.numpy as jnp
from jax import lax

NY = 1024
SRC = 8
KD = 4
ITERS = 8
ELEC = 64
KNUM = 16
NX = 1024


def draw_sweep_counts(key, part):
    keys = jax.random.split(key, 4)
    groups = KNUM // KD
    index = jnp.arange(KNUM, dtype=jnp.int32)
    heavy = jax.random.randint(keys[0], (), 0, groups)
    high = jax.random.randint(keys[1], (KNUM,), ITERS // 2 + 2, ITERS + 1)
    low = jax.random.randint(keys[2], (KNUM,), 1, ITERS // 2)
    counts = jnp.where(index // KD == heavy, high, low)
    top = heavy * KD + jax.random.randint(keys[3], (), 0, KD)
    bottom = (heavy + 1) % groups * KD
    counts = jnp.where(index == top, ITERS, counts)
    counts = jnp.where(index == bottom, 1, counts)
    return counts.astype(jnp.int32)


def draw_source_pairs(key, part):
    keys = jax.random.split(key, 2)
    first = jax.random.randint(keys[0], (SRC,), 0, ELEC)
    offset = jax.random.randint(keys[1], (SRC,), 1, ELEC)
    second = (first + offset) % ELEC
    return jnp.stack([first, second], axis=1).astype(jnp.int32)


def set_ends(values, stream_key, smallest, high):
    place = [jax.random.randint(jax.random.fold_in(stream_key, axis), (), 0, length) for axis, length in enumerate(values.shape)]
    main_axis = values.shape.index(max(values.shape))
    next_to = place[:main_axis] + [(place[main_axis] + 1) % values.shape[main_axis]] + place[main_axis + 1:]
    return values.at[tuple(place)].set(smallest).at[tuple(next_to)].set(high)


def steps_of(stream_key, extent, pieces, low, high):
    def one(axis_at, shards_of):
        steps = jax.random.uniform(jax.random.fold_in(jax.random.fold_in(stream_key, 6), axis_at), (shards_of,), jnp.float32, low / len(pieces), high / len(pieces))
        return jnp.repeat(jnp.exp(steps), extent[axis_at] // shards_of).reshape((-1,) + (1,) * (len(extent) - axis_at - 1))

    level = one(*pieces[0])
    for cut in pieces[1:]:
        level = level * one(*cut)
    return level


def noise(rng, shape, spread, most, cuts=(), held_as=jnp.bfloat16):
    result = jax.random.normal(rng, shape, jnp.float32) * spread
    if len(cuts) > 0:
        result = steps_of(rng, shape, cuts, -0.22, 0.18) * result
    return jnp.clip(result, min=-most, max=most).astype(held_as)


def setup_inputs(seed: int = 0) -> dict:
    arg_keys = jax.random.split(jax.random.key(seed), 8)
    return {
        "initial_fields": noise(arg_keys[0], (KNUM, SRC, NX, NY), 1.0, 6.0, ((0, 4), (2, 32))),
        "conductivity": jnp.clip(jnp.exp(math.log(10.0) - 4.6051702 * jax.random.uniform(arg_keys[1], (NX, NY), jnp.float32) ** steps_of(arg_keys[1], (NX, NY), ((0, 32),), -0.2, 0.2)), 0.1, 10.0),
        "wavenumbers": jnp.clip(jnp.exp(jax.random.uniform(arg_keys[2], (KNUM,), jnp.float32, math.log(0.05), math.log(1.5))), 0.05, 1.5),
        "quad_weights": jnp.clip(jnp.exp(jax.random.uniform(arg_keys[3], (KNUM,), jnp.float32, math.log(0.05), math.log(0.3))), 0.05, 0.3),
        "sweep_counts": draw_sweep_counts(jax.random.fold_in(arg_keys[7], 71), 0),
        "electrode_cells": set_ends(jax.random.randint(arg_keys[5], (ELEC,), 0, NX), jax.random.fold_in(arg_keys[5], 1), 0, NX - 1).astype(jnp.int32),
        "source_pairs": draw_source_pairs(jax.random.fold_in(arg_keys[7], 71), 0),
    }


LOWER = 0.1
UPPER = 2.0
THETA = (UPPER + LOWER) / 2.0
DELTA = (UPPER - LOWER) / 2.0
SIGMA_ONE = THETA / DELTA
CURRENT = 2.0


def face_values(conductivity):
    padded = jnp.pad(conductivity, 1)
    face_north = 0.5 * (conductivity + padded[:-2, 1:-1])
    face_south = 0.5 * (conductivity + padded[2:, 1:-1])
    face_west = 0.5 * (conductivity + padded[1:-1, :-2])
    face_east = 0.5 * (conductivity + padded[1:-1, 2:])
    return face_north, face_south, face_west, face_east


def neighbours(padded_rows, facets):
    face_north, face_south, face_west, face_east = facets
    centre = padded_rows[:, 1:-1]
    columns = jnp.pad(centre, ((0, 0), (0, 0), (1, 1)))
    total = face_north * padded_rows[:, :-2] + face_south * padded_rows[:, 2:]
    return total + face_west * columns[:, :, :-2] + face_east * columns[:, :, 2:]


def chebyshev_step(step, field, direction, rho_prev, residual, diag_k, active):
    scaled = residual / diag_k
    rho_next = 1.0 / (2.0 * SIGMA_ONE - rho_prev)
    first = step == 0
    keep = jnp.where(first, 0.0, rho_next * rho_prev)
    gain = jnp.where(first, 1.0 / THETA, 2.0 * rho_next / DELTA)
    moved = keep * direction + gain * scaled
    new_rho = jnp.where(first, 1.0 / SIGMA_ONE, rho_next)
    return (jnp.where(active, field + moved, field), jnp.where(active, moved, direction), jnp.where(active, new_rho, rho_prev))


def reference(initial_fields, conductivity, wavenumbers, quad_weights, sweep_counts, electrode_cells, source_pairs):
    facets = face_values(conductivity)
    diagonal = facets[0] + facets[1] + facets[2] + facets[3]
    row_ids = jnp.arange(NX, dtype=jnp.int32)
    column_one = (jnp.arange(NY, dtype=jnp.int32) == 0).astype(jnp.float32)
    electrode_rows = electrode_cells[source_pairs]
    positive = (row_ids[None, :] == electrode_rows[:, 0:1]).astype(jnp.float32)
    negative = (row_ids[None, :] == electrode_rows[:, 1:2]).astype(jnp.float32)
    sources = CURRENT * (positive - negative)[:, :, None] * column_one[None, None, :]

    def per_wave(summed, item):
        field_start, wavenumber, weight, count = item
        diag_k = diagonal + wavenumber * wavenumber * conductivity

        def sweep(step, carry):
            field_now, dir_now, rho_now = carry
            padded = jnp.pad(field_now, ((0, 0), (1, 1), (0, 0)))
            residual = sources - (diag_k * field_now - neighbours(padded, facets))
            return chebyshev_step(step, field_now, dir_now, rho_now, residual, diag_k, True)

        start = field_start.astype(jnp.float32)
        rho_start = jnp.full((start.shape[0], 1, 1), 1.0 / SIGMA_ONE, jnp.float32)
        solved = lax.fori_loop(0, count, sweep, (start, jnp.zeros_like(start), rho_start))[0]
        return summed + weight * solved, None

    summed, _ = lax.scan(per_wave, jnp.zeros((SRC, NX, NY), jnp.float32), (initial_fields, wavenumbers, quad_weights, sweep_counts))
    return summed
```

```python
import functools

import jax
import jax.numpy as jnp
from jax import lax
from jax.experimental import pallas as pl
from jax.experimental.pallas import tpu as pltpu
from jax.sharding import PartitionSpec as P

ITERS = 8
LOWER = 0.1
UPPER = 2.0
THETA = (UPPER + LOWER) / 2.0
DELTA = (UPPER - LOWER) / 2.0
SIGMA_ONE = THETA / DELTA
CURRENT = 2.0

TAU = [1.0, SIGMA_ONE]
for _ in range(ITERS):
    TAU.append(2.0 * SIGMA_ONE * TAU[-1] - TAU[-2])
OMEGA = 2.0 * (THETA - 1.0) / DELTA

LANES = 128
ROWS = 32
PAD = 16
SPAN = ROWS + 2 * PAD
SWEEP_ROWS = ((8, 6), (8, 6), (8, 6), (12, 5), (12, 5), (12, 5), (12, 5), (16, 4))
MESH = pl.DeviceIdType.MESH


def chosen(index, table):
    value = jnp.float32(0.0)
    for position, entry in enumerate(table):
        value = jnp.where(index == position, jnp.float32(entry), value)
    return value


def slot_column(pair, half, wave_pos):
    middle = jnp.logical_or(pair == 1, pair == 2)
    ahead = jnp.where(pair == 0, 2, jnp.where(middle, 1 + 2 * half, 0))
    offset = jnp.where(middle, pair - 1, half)
    return 2 * lax.rem(wave_pos + ahead, 4) + offset


def kernel(
    fields, sigma, wavenumbers, weights, counts, electrodes, pairs, out,
    halo_n, halo_s, sig_n, sig_s, sig, w, coef, gain, src, acc, from_low, from_high,
    omegas, charges, finals, h_send, h_recv, s_send, s_recv, r_send, r_recv,
):
    per_group = fields.shape[0]
    tiles = fields.shape[3] // LANES
    tile_count = lax.axis_size("tile")
    wave_count = lax.axis_size("wave")
    tile_pos = lax.axis_index("tile")
    wave_pos = lax.axis_index("wave")
    south = {"tile": lax.rem(tile_pos + 1, tile_count)}
    north = {"tile": lax.rem(tile_pos + tile_count - 1, tile_count)}
    above = {"wave": lax.rem(wave_pos + 1, wave_count)}
    below = {"wave": lax.rem(wave_pos + wave_count - 1, wave_count)}

    barrier = pltpu.get_barrier_semaphore()
    for other in (south, north, above, below):
        pl.semaphore_signal(barrier, inc=1, device_id=other, device_id_type=MESH)
    pl.semaphore_wait(barrier, 4)

    def remote(source, target, send, recv, device):
        return pltpu.make_async_remote_copy(
            src_ref=source, dst_ref=target, send_sem=send, recv_sem=recv,
            device_id=device, device_id_type=MESH,
        )

    sig_south = remote(sigma.at[pl.ds(ROWS - 8, 8)], sig_n, s_send.at[0], s_recv.at[0], south)
    sig_north = remote(sigma.at[pl.ds(0, 8)], sig_s, s_send.at[1], s_recv.at[1], north)
    sig_south.start()
    sig_north.start()

    def halo_copies(slot, k):
        column = slot_column(slot // 2, lax.rem(slot, 2), wave_pos)
        return (
            remote(fields.at[k, column, pl.ds(ROWS - 16, 16)], halo_n.at[slot, k],
                   h_send.at[0, slot, k], h_recv.at[0, slot, k], south),
            remote(fields.at[k, column, pl.ds(0, 16)], halo_s.at[slot, k],
                   h_send.at[1, slot, k], h_recv.at[1, slot, k], north),
        )

    @pl.loop(0, 4)
    def _(pair):
        @pl.loop(0, per_group)
        def _(k):
            for half in range(2):
                for copy in halo_copies(2 * pair + half, k):
                    copy.start()

    for k in range(per_group):
        count = counts[wave_pos * per_group + k]
        for step in range(ITERS):
            live = step - (ITERS - count)
            omegas[k * ITERS + step] = jnp.where(
                live < 0, jnp.float32(2.0),
                jnp.where(live == 0, jnp.float32(1.0 + 0.5 * OMEGA), jnp.float32(OMEGA)))
            charges[k * ITERS + step] = chosen(live, [0.5] + TAU[1:ITERS])
        finals[k] = weights[wave_pos * per_group + k] * chosen(
            count, [1.0 / tau for tau in TAU[: ITERS + 1]])

    lane = lax.broadcasted_iota(jnp.int32, (8, LANES), 1)
    sub = lax.broadcasted_iota(jnp.int32, (8, LANES), 0)
    first_lane = lane == 0
    last_lane = lane == LANES - 1
    zero = jnp.zeros((8, LANES), jnp.float32)

    for tile in range(tiles):
        for edge in (0, SPAN - 8):
            sig[tile, pl.ds(edge, 8), :] = zero + 1.0
            for half in range(2):
                for buf in range(2):
                    w[buf, half, tile, pl.ds(edge, 8), :] = zero
        for row in range(8, SPAN - 8, 8):
            for face in range(4):
                coef[0, face, tile, pl.ds(row, 8), :] = zero
        for row in range(0, ROWS, 8):
            sig[tile, pl.ds(PAD + row, 8), :] = sigma[pl.ds(row, 8), pl.ds(tile * LANES, LANES)]
            for slot in range(8):
                acc[slot, tile, pl.ds(row, 8), :] = zero
    sig_south.wait_recv()
    sig_north.wait_recv()
    for tile in range(tiles):
        sig[tile, pl.ds(8, 8), :] = sig_n[:, pl.ds(tile * LANES, LANES)]
        sig[tile, pl.ds(PAD + ROWS, 8), :] = sig_s[:, pl.ds(tile * LANES, LANES)]

    def beside(values, tile):
        left = pltpu.roll(values[tile], 1, 1)
        right = pltpu.roll(values[tile], LANES - 1, 1)
        if tile > 0:
            left = jnp.where(first_lane, pltpu.roll(values[tile - 1], 1, 1), left)
        if tile < tiles - 1:
            right = jnp.where(last_lane, pltpu.roll(values[tile + 1], LANES - 1, 1), right)
        return left, right

    @pl.loop(1, SPAN // 8 - 1)
    def _(row_tile):
        row = pl.multiple_of(row_tile * 8, 8)
        place = tile_pos * ROWS + row - PAD + sub
        top = place == 0
        bottom = place == tile_count * ROWS - 1
        centre = [sig[tile, pl.ds(row, 8), :] for tile in range(tiles)]
        for tile in range(tiles):
            mid = centre[tile]
            left, right = beside(centre, tile)
            up = jnp.where(top, 0.0, sig[tile, pl.ds(row - 1, 8), :])
            down = jnp.where(bottom, 0.0, sig[tile, pl.ds(row + 1, 8), :])
            if tile == 0:
                left = jnp.where(first_lane, 0.0, left)
            if tile == tiles - 1:
                right = jnp.where(last_lane, 0.0, right)
            faces = [0.5 * (mid + near) for near in (up, down, left, right)]
            diagonal = (faces[0] + faces[1]) + (faces[2] + faces[3])
            faces[0] = jnp.where(top, 0.0, faces[0])
            faces[1] = jnp.where(bottom, 0.0, faces[1])
            if tile == 0:
                faces[2] = jnp.where(first_lane, 0.0, faces[2])
            if tile == tiles - 1:
                faces[3] = jnp.where(last_lane, 0.0, faces[3])
            for k in range(per_group):
                number = wavenumbers[wave_pos * per_group + k]
                scale = (2.0 / DELTA) / (diagonal + (number * number) * mid)
                if tile == 0:
                    gain[k, pl.ds(row, 8), :] = scale
                for face in range(4):
                    value = faces[face] * scale
                    coef[2 + 2 * k, face, tile, pl.ds(row, 8), :] = value
                    coef[1 + 2 * k, face, tile, pl.ds(row, 8), :] = 0.5 * value

    def sweep(step, k, pair):
        start, count = SWEEP_ROWS[step]
        now, later = step % 2, (step + 1) % 2
        live = step - (ITERS - counts[wave_pos * per_group + k])
        table = jnp.where(live < 0, 0, jnp.where(live == 0, 1 + 2 * k, 2 + 2 * k))
        omega = omegas[k * ITERS + step]
        charge = charges[k * ITERS + step]
        final = finals[k]

        for row_tile in range(count):
            row = start + 8 * row_tile
            centre = [[w[now, half, tile, pl.ds(row, 8), :] for tile in range(tiles)] for half in range(2)]
            for tile in range(tiles):
                c_n, c_s, c_w, c_e = [coef[table, face, tile, pl.ds(row, 8), :] for face in range(4)]
                for half in range(2):
                    mid = centre[half][tile]
                    left, right = beside(centre[half], tile)
                    before = mid if step == 0 else w[later, half, tile, pl.ds(row, 8), :]
                    up = w[now, half, tile, pl.ds(row - 1, 8), :]
                    down = w[now, half, tile, pl.ds(row + 1, 8), :]
                    value = ((omega * mid - before) + (c_n * up + c_s * down)) + (c_w * left + c_e * right)
                    if tile == 0:
                        value = value + charge * src[half, pl.ds(row, 8), :]
                    if step == ITERS - 1:
                        acc[2 * pair + half, tile, pl.ds(row - PAD, 8), :] += final * value
                    else:
                        w[later, half, tile, pl.ds(row, 8), :] = value

    def rs_copies(pair):
        slot = 2 * pair
        return (
            remote(acc.at[slot], from_low.at[pair], r_send.at[0, pair], r_recv.at[0, pair], above),
            remote(acc.at[slot + 1], from_high.at[pair], r_send.at[1, pair], r_recv.at[1, pair], below),
        )

    @pl.loop(0, 4)
    def _(pair):
        columns = [slot_column(pair, half, wave_pos) for half in range(2)]

        @pl.loop(0, per_group)
        def _(k):
            for half in range(2):
                for copy in halo_copies(2 * pair + half, k):
                    copy.wait_recv()
            for half in range(2):
                slot = 2 * pair + half
                low = electrodes[pairs[columns[half], 0]] - tile_pos * ROWS + PAD
                high = electrodes[pairs[columns[half], 1]] - tile_pos * ROWS + PAD
                for row in range(8, SPAN - 8, 8):
                    spot = jnp.where(row + sub == low, CURRENT, 0.0) - jnp.where(row + sub == high, CURRENT, 0.0)
                    src[half, pl.ds(row, 8), :] = jnp.where(first_lane, spot * gain[k, pl.ds(row, 8), :], 0.0)
                for tile in range(tiles):
                    cut = pl.ds(tile * LANES, LANES)
                    w[0, half, tile, pl.ds(8, 8), :] = halo_n[slot, k, :, cut].astype(jnp.float32)[8:]
                    for row in range(0, ROWS, 16):
                        w[0, half, tile, pl.ds(PAD + row, 16), :] = fields[
                            k, columns[half], pl.ds(row, 16), cut].astype(jnp.float32)
                    w[0, half, tile, pl.ds(PAD + ROWS, 8), :] = halo_s[slot, k, :, cut].astype(jnp.float32)[:8]
            for step in range(ITERS):
                sweep(step, k, pair)

        @pl.when(pair == 1)
        def _():
            rs_copies(0)[0].wait_recv()
            acc[2] += from_low[0]

        @pl.when(pair == 2)
        def _():
            rs_copies(0)[1].wait_recv()
            acc[5] += from_high[0]

        @pl.when(pair < 3)
        def _():
            for copy in rs_copies(pair):
                copy.start()

    for pair in (1, 2):
        for copy in rs_copies(pair):
            copy.wait_recv()
    for half in range(2):
        for tile in range(tiles):
            for row in range(0, ROWS, 8):
                cut = pl.ds(row, 8)
                out[half, cut, pl.ds(tile * LANES, LANES)] = (
                    acc[6 + half, tile, cut, :] + (from_low[1 + half, tile, cut, :] + from_high[1 + half, tile, cut, :]))

    for pair in range(3):
        for copy in rs_copies(pair):
            copy.wait_send()
    sig_south.wait_send()
    sig_north.wait_send()

    @pl.loop(0, 8)
    def _(slot):
        @pl.loop(0, per_group)
        def _(k):
            for copy in halo_copies(slot, k):
                copy.wait_send()


def local(fields, sigma, wavenumbers, weights, counts, electrodes, pairs):
    per_group, sources, rows, depth = fields.shape
    tiles = depth // LANES
    vmem = pl.BlockSpec(memory_space=pltpu.VMEM)
    smem = pl.BlockSpec(memory_space=pltpu.SMEM)
    f32 = jnp.float32
    return pl.pallas_call(
        kernel,
        out_shape=jax.ShapeDtypeStruct((sources // 4, rows, depth), f32),
        in_specs=[vmem, vmem, smem, smem, smem, smem, smem],
        out_specs=vmem,
        scratch_shapes=[
            pltpu.VMEM((sources, per_group, 16, depth), jnp.bfloat16),
            pltpu.VMEM((sources, per_group, 16, depth), jnp.bfloat16),
            pltpu.VMEM((8, depth), f32),
            pltpu.VMEM((8, depth), f32),
            pltpu.VMEM((tiles, SPAN, LANES), f32),
            pltpu.VMEM((2, 2, tiles, SPAN, LANES), f32),
            pltpu.VMEM((1 + 2 * per_group, 4, tiles, SPAN, LANES), f32),
            pltpu.VMEM((per_group, SPAN, LANES), f32),
            pltpu.VMEM((2, SPAN, LANES), f32),
            pltpu.VMEM((sources, tiles, rows, LANES), f32),
            pltpu.VMEM((3, tiles, rows, LANES), f32),
            pltpu.VMEM((3, tiles, rows, LANES), f32),
            pltpu.SMEM((per_group * ITERS,), f32),
            pltpu.SMEM((per_group * ITERS,), f32),
            pltpu.SMEM((per_group,), f32),
            pltpu.SemaphoreType.DMA((2, sources, per_group)),
            pltpu.SemaphoreType.DMA((2, sources, per_group)),
            pltpu.SemaphoreType.DMA((2,)),
            pltpu.SemaphoreType.DMA((2,)),
            pltpu.SemaphoreType.DMA((2, 3)),
            pltpu.SemaphoreType.DMA((2, 3)),
        ],
        compiler_params=pltpu.CompilerParams(
            collective_id=0, has_side_effects=True, vmem_limit_bytes=40 * 1024 * 1024),
    )(fields, sigma, wavenumbers, weights, counts, electrodes, pairs)


def solution(mesh):
    placed = (P("wave", None, "tile", None), P("tile", None), P(), P(), P(), P(), P())
    return jax.shard_map(
        local, mesh=mesh, in_specs=placed, out_specs=P("wave", "tile", None), check_vma=False
    )
```

```python
import jax
import jax.numpy as jnp
from jax import lax
from jax.experimental import pallas as pl
from jax.experimental.pallas import tpu as pltpu
from jax.sharding import PartitionSpec as P

ITERS = 8
LOWER = 0.1
UPPER = 2.0
THETA = (UPPER + LOWER) / 2.0
DELTA = (UPPER - LOWER) / 2.0
SIGMA_ONE = THETA / DELTA
CURRENT = 2.0

TAU = [1.0, SIGMA_ONE]
for _ in range(ITERS):
    TAU.append(2.0 * SIGMA_ONE * TAU[-1] - TAU[-2])
OMEGA = 2.0 * (THETA - 1.0) / DELTA

LANES = 128
SUBS = 8
PARTS = 8
ROWS = 32
HALO = 8
HELD = ROWS + 2 * HALO
SPAN = 64
FIRST = 8
CORE = FIRST + HALO
LAST = FIRST + HELD
UNROLL = 4
MESH = pl.DeviceIdType.MESH
F32 = jnp.float32
BF16 = jnp.bfloat16


def chosen(index, table):
    value = jnp.float32(0.0)
    for position, entry in enumerate(table):
        value = jnp.where(index == position, jnp.float32(entry), value)
    return value


def slot_column(pair, half, wave_pos):
    middle = jnp.logical_or(pair == 1, pair == 2)
    ahead = jnp.where(pair == 0, 2, jnp.where(middle, 1 + 2 * half, 0))
    offset = jnp.where(middle, pair - 1, half)
    return 2 * lax.rem(wave_pos + ahead, 4) + offset


def thirds(values):
    high = values.astype(BF16)
    rest = values - high.astype(F32)
    middle = rest.astype(BF16)
    low = (rest - middle.astype(F32)).astype(BF16)
    return high, middle, low


def kernel(
    fields_in, sigma_in, wavenumbers_in, weights_in, counts_in, electrodes_in, pairs_in, out,
    fields, sigma, wavenumbers, weights, counts, electrodes, pairs,
    into, back, stage, sig_n, sig_s, sig, diag, face_n, face_w,
    an, aw, root, inverse, vectors, src, w, zbuf, acc, from_low, from_high,
    in_sem, h_send, h_recv, s_send, s_recv, r_send, r_recv,
):
    per_group = fields.shape[0]
    tile_count = lax.axis_size("tile")
    wave_count = lax.axis_size("wave")
    tile_pos = lax.axis_index("tile")
    wave_pos = lax.axis_index("wave")
    south = {"tile": lax.rem(tile_pos + 1, tile_count)}
    north = {"tile": lax.rem(tile_pos + tile_count - 1, tile_count)}
    above = {"wave": lax.rem(wave_pos + 1, wave_count)}
    below = {"wave": lax.rem(wave_pos + wave_count - 1, wave_count)}

    barrier = pltpu.get_barrier_semaphore()
    for other in (south, north, above, below):
        pl.semaphore_signal(barrier, inc=1, device_id=other, device_id_type=MESH)

    loads = [
        pltpu.make_async_copy(source, target, in_sem.at[place])
        for place, (source, target) in enumerate((
            (fields_in, fields), (sigma_in, sigma), (wavenumbers_in, wavenumbers), (weights_in, weights),
            (counts_in, counts), (electrodes_in, electrodes), (pairs_in, pairs)))
    ]
    for load in loads:
        load.start()

    lane = lax.broadcasted_iota(jnp.int32, (SUBS, LANES), 1)
    sub = lax.broadcasted_iota(jnp.int32, (SUBS, LANES), 0)
    first_lane = lane == 0
    last_lane = lane == LANES - 1
    zero = jnp.zeros((SUBS, LANES), F32)

    @pl.loop(0, PARTS)
    def _(block):
        wide = PARTS * LANES
        base = pl.multiple_of(block * LANES, LANES)
        row = lax.broadcasted_iota(jnp.int32, (LANES, wide), 0) + base
        column = lax.broadcasted_iota(jnp.int32, (LANES, wide), 1)
        into[pl.ds(base, LANES), :] = jnp.where(
            row == lax.rem(column, LANES) * PARTS + lax.div(column, LANES), 1.0, 0.0).astype(BF16)
        back[pl.ds(base, LANES), :] = jnp.where(
            column == lax.rem(row, LANES) * PARTS + lax.div(row, LANES), 1.0, 0.0).astype(BF16)

    for part in range(PARTS):
        rows8 = pl.ds(part * SUBS, SUBS)
        for row in range(LAST, SPAN):
            an[row, rows8, :] = zero
            aw[row, rows8, :] = zero
            src[row] = zero
            for buf in range(2):
                w[buf, row, rows8, :] = zero
        for edge in (0, LAST):
            sig[part, pl.ds(edge, FIRST), :] = zero + 1.0

    for load in loads:
        load.wait()
    pl.semaphore_wait(barrier, 4)

    def remote(source, target, send, recv, device):
        return pltpu.make_async_remote_copy(
            src_ref=source, dst_ref=target, send_sem=send, recv_sem=recv,
            device_id=device, device_id_type=MESH,
        )

    sig_south = remote(sigma.at[pl.ds(ROWS - HALO, HALO)], sig_n, s_send.at[0], s_recv.at[0], south)
    sig_north = remote(sigma.at[pl.ds(0, HALO)], sig_s, s_send.at[1], s_recv.at[1], north)
    sig_south.start()
    sig_north.start()

    def halo_copies(pair):
        return (
            remote(stage.at[pair, :, :, pl.ds(ROWS, HALO)], stage.at[pair, :, :, pl.ds(0, HALO)],
                   h_send.at[0, pair], h_recv.at[0, pair], south),
            remote(stage.at[pair, :, :, pl.ds(HALO, HALO)], stage.at[pair, :, :, pl.ds(HALO + ROWS, HALO)],
                   h_send.at[1, pair], h_recv.at[1, pair], north),
        )

    @pl.loop(0, 4)
    def _(pair):
        columns = [slot_column(pair, half, wave_pos) for half in range(2)]
        block = jnp.concatenate(
            [fields[k, columns[half]] for half in range(2) for k in range(per_group)], axis=0)
        moved = jnp.dot(block, into[...], preferred_element_type=F32)
        for part in range(PARTS):
            for place in range(SUBS):
                stage[pair, part, place, pl.ds(HALO, ROWS), :] = moved[
                    place * ROWS:(place + 1) * ROWS, part * LANES:(part + 1) * LANES]
        for copy in halo_copies(pair):
            copy.start()

    def by_wavenumber(scalars):
        value = zero
        for k, scalar in enumerate(scalars):
            value = jnp.where(lax.rem(sub, per_group) == k, scalar, value)
        return value

    group = [wave_pos * per_group + k for k in range(per_group)]
    square = by_wavenumber([wavenumbers[g] * wavenumbers[g] for g in group])
    final = by_wavenumber([
        weights[g] * chosen(counts[g], [1.0 / tau for tau in TAU[: ITERS + 1]]) for g in group])
    for step in range(ITERS):
        live = [step - (ITERS - counts[g]) for g in group]
        vectors[3 * step] = by_wavenumber([
            jnp.where(at < 0, F32(2.0), jnp.where(at == 0, F32(1.0 + 0.5 * OMEGA), F32(OMEGA))) for at in live])
        vectors[3 * step + 1] = by_wavenumber([
            jnp.where(at < 0, F32(0.0), jnp.where(at == 0, F32(0.5), F32(1.0))) for at in live])
        vectors[3 * step + 2] = by_wavenumber([chosen(at, [0.5] + TAU[1:ITERS]) for at in live])

    sig_south.wait_recv()
    sig_north.wait_recv()
    whole = jnp.concatenate([sig_n[...], sigma[...], sig_s[...]], axis=0)
    moved = jnp.dot(jnp.concatenate(thirds(whole), axis=0), into[...], preferred_element_type=F32)
    moved = (moved[:HELD] + moved[HELD:2 * HELD]) + moved[2 * HELD:]
    for part in range(PARTS):
        sig[part, pl.ds(FIRST, HELD), :] = moved[:, part * LANES:(part + 1) * LANES]

    @pl.loop(1, LAST // SUBS)
    def _(row_tile):
        row = pl.multiple_of(row_tile * SUBS, SUBS)
        place = tile_pos * ROWS + row - CORE + sub
        last_row = tile_count * ROWS
        centre = [sig[part, pl.ds(row, SUBS), :] for part in range(PARTS)]
        for part in range(PARTS):
            mid = centre[part]
            up = jnp.where(place == 0, 0.0, sig[part, pl.ds(row - 1, SUBS), :])
            down = jnp.where(place == last_row - 1, 0.0, sig[part, pl.ds(row + 1, SUBS), :])
            if part == 0:
                left = jnp.where(first_lane, 0.0, pltpu.roll(centre[-1], 1, 1))
            else:
                left = centre[part - 1]
            if part == PARTS - 1:
                right = jnp.where(last_lane, 0.0, pltpu.roll(centre[0], LANES - 1, 1))
            else:
                right = centre[part + 1]
            faces = [0.5 * (mid + near) for near in (up, down, left, right)]
            diag[part, pl.ds(row, SUBS), :] = (faces[0] + faces[1]) + (faces[2] + faces[3])
            outside = jnp.logical_or(place == 0, place == last_row)
            face_n[part, pl.ds(row, SUBS), :] = jnp.where(outside, 0.0, (2.0 / DELTA) * faces[0])
            west = (2.0 / DELTA) * faces[2]
            if part == 0:
                west = jnp.where(first_lane, 0.0, west)
            face_w[part, pl.ds(row, SUBS), :] = west

    def couplings(row, above_row):
        def spread(ref, part):
            return jnp.broadcast_to(ref[part, pl.ds(row, 1), :], (SUBS, LANES))

        here = []
        for part in range(PARTS):
            rows8 = pl.ds(part * SUBS, SUBS)
            value = spread(diag, part) + square * spread(sig, part)
            guess = lax.rsqrt(value)
            guess = guess * (1.5 - (0.5 * value) * (guess * guess))
            root[row, rows8, :] = value * guess
            inverse[row, rows8, :] = guess
            an[row, rows8, :] = spread(face_n, part) * (guess * above_row[part])
            here.append(guess)
        for part in range(PARTS):
            beside = here[part - 1] if part else pltpu.roll(here[-1], 1, 1)
            aw[row, pl.ds(part * SUBS, SUBS), :] = spread(face_w, part) * (here[part] * beside)
        return tuple(here)

    lax.fori_loop(FIRST, LAST, couplings, (zero,) * PARTS)

    def sweep(step):
        now, later = step % 2, (step + 1) % 2
        before = now if step == 0 else later
        centre_gain = vectors[3 * step]
        side_gain = vectors[3 * step + 1]
        charge = vectors[3 * step + 2]
        start = FIRST + step + 1
        blocks = -(-(HELD - 1 - 2 * step) // UNROLL)
        parts = [pl.ds(part * SUBS, SUBS) for part in range(PARTS)]

        def one(row, carry):
            old, sums = carry
            u = [w[now, row, at, :] for at in parts]
            north_c = [an[row, at, :] for at in parts]
            west_c = [aw[row, at, :] for at in parts]
            for part, at in enumerate(parts):
                value = side_gain * (sums[part] + north_c[part] * u[part]) + (
                    centre_gain * old[part] - w[before, row - 1, at, :])
                if part == 0:
                    value = value + charge * src[row - 1]
                w[later, row - 1, at, :] = value
            flows = [west_c[part] * u[part] for part in range(PARTS)]
            left = [pltpu.roll(u[-1], 1, 1)] + u[:-1]
            right = flows[1:] + [pltpu.roll(flows[0], LANES - 1, 1)]
            sums = [north_c[part] * old[part] + (west_c[part] * left[part] + right[part]) for part in range(PARTS)]
            return tuple(u), tuple(sums)

        def body(block, carry):
            for place in range(UNROLL):
                carry = one(start + UNROLL * block + place, carry)
            return carry

        opening = tuple(w[now, start - 1, at, :] for at in parts)
        lax.fori_loop(0, blocks, body, (opening, (zero,) * PARTS))

    def rs_copies(pair):
        slot = 2 * pair
        return (
            remote(acc.at[slot], from_low.at[pair], r_send.at[0, pair], r_recv.at[0, pair], above),
            remote(acc.at[slot + 1], from_high.at[pair], r_send.at[1, pair], r_recv.at[1, pair], below),
        )

    flat = stage.reshape(4 * PARTS, SUBS * HELD, LANES)

    @pl.loop(0, 4)
    def _(pair):
        columns = [slot_column(pair, half, wave_pos) for half in range(2)]
        spots = []
        for end in range(2):
            low, high = [electrodes[pairs[column, end]] for column in columns]
            spots.append(jnp.where(sub < per_group, low, high) - tile_pos * ROWS + CORE)
        for copy in halo_copies(pair):
            copy.wait_recv()

        @pl.loop(FIRST, LAST)
        def _(row):
            for part in range(PARTS):
                rows8 = pl.ds(part * SUBS, SUBS)
                given = flat[pair * PARTS + part, pl.ds(row - FIRST, SUBS, HELD), :]
                w[0, row, rows8, :] = given * root[row, rows8, :]
            spot = jnp.where(row == spots[0], CURRENT, 0.0) - jnp.where(row == spots[1], CURRENT, 0.0)
            spot = (2.0 / DELTA) * spot * inverse[row, pl.ds(0, SUBS), :]
            src[row] = jnp.where(first_lane, spot, 0.0)

        for step in range(ITERS):
            sweep(step)

        @pl.loop(0, ROWS)
        def _(row):
            for part in range(PARTS):
                rows8 = pl.ds(part * SUBS, SUBS)
                zbuf[part, pl.ds(row, SUBS, ROWS), :] = (final * inverse[CORE + row, rows8, :]) * w[
                    ITERS % 2, CORE + row, rows8, :]

        for half in range(2):
            for part in range(PARTS):
                for row in range(0, ROWS, SUBS):
                    terms = [zbuf[part, pl.ds((half * per_group + k) * ROWS + row, SUBS), :] for k in range(per_group)]
                    acc[2 * pair + half, part, pl.ds(row, SUBS), :] = (terms[0] + terms[1]) + (terms[2] + terms[3])

        @pl.when(pair == 1)
        def _():
            rs_copies(0)[0].wait_recv()
            acc[2] += from_low[0]

        @pl.when(pair == 2)
        def _():
            rs_copies(0)[1].wait_recv()
            acc[5] += from_high[0]

        @pl.when(pair < 3)
        def _():
            for copy in rs_copies(pair):
                copy.start()

    for pair in (1, 2):
        for copy in rs_copies(pair):
            copy.wait_recv()
    total = jnp.concatenate([
        jnp.concatenate([acc[6 + half, part] + (from_low[1 + half, part] + from_high[1 + half, part])
                         for part in range(PARTS)], axis=1)
        for half in range(2)], axis=0)
    moved = jnp.dot(jnp.concatenate(thirds(total), axis=0), back[...], preferred_element_type=F32)
    for half in range(2):
        cut = half * ROWS
        out[half] = (moved[cut:cut + ROWS] + moved[2 * ROWS + cut:3 * ROWS + cut]) + moved[
            4 * ROWS + cut:5 * ROWS + cut]

    for pair in range(3):
        for copy in rs_copies(pair):
            copy.wait_send()
    for pair in range(4):
        for copy in halo_copies(pair):
            copy.wait_send()
    sig_south.wait_send()
    sig_north.wait_send()


def local(*arrays):
    fields = arrays[0]
    per_group, sources, rows, depth = fields.shape
    small = [pltpu.SMEM(a.shape, a.dtype) for a in arrays[2:]]
    tall = pltpu.VMEM((SPAN, PARTS * SUBS, LANES), F32)
    flat = pltpu.VMEM((PARTS, SPAN, LANES), F32)
    return pl.pallas_call(
        kernel,
        out_shape=jax.ShapeDtypeStruct((sources // 4, rows, depth), F32),
        in_specs=[pl.BlockSpec(memory_space=pl.ANY)] * len(arrays),
        out_specs=pl.BlockSpec(memory_space=pltpu.VMEM),
        scratch_shapes=[
            pltpu.VMEM(fields.shape, fields.dtype),
            pltpu.VMEM((rows, depth), F32),
            *small,
            pltpu.VMEM((depth, depth), BF16),
            pltpu.VMEM((depth, depth), BF16),
            pltpu.VMEM((4, PARTS, SUBS, HELD, LANES), F32),
            pltpu.VMEM((HALO, depth), F32),
            pltpu.VMEM((HALO, depth), F32),
            flat, flat, flat, flat,
            tall, tall, tall, tall,
            pltpu.VMEM((3 * ITERS, SUBS, LANES), F32),
            pltpu.VMEM((SPAN, SUBS, LANES), F32),
            pltpu.VMEM((2, SPAN, PARTS * SUBS, LANES), F32),
            pltpu.VMEM((PARTS, SUBS * ROWS, LANES), F32),
            pltpu.VMEM((sources, PARTS, rows, LANES), F32),
            pltpu.VMEM((3, PARTS, rows, LANES), F32),
            pltpu.VMEM((3, PARTS, rows, LANES), F32),
            pltpu.SemaphoreType.DMA((7,)),
            pltpu.SemaphoreType.DMA((2, 4)),
            pltpu.SemaphoreType.DMA((2, 4)),
            pltpu.SemaphoreType.DMA((2,)),
            pltpu.SemaphoreType.DMA((2,)),
            pltpu.SemaphoreType.DMA((2, 3)),
            pltpu.SemaphoreType.DMA((2, 3)),
        ],
        compiler_params=pltpu.CompilerParams(
            collective_id=0, has_side_effects=True, vmem_limit_bytes=48 * 1024 * 1024),
    )(*arrays)


def solution(mesh):
    placed = (P("wave", None, "tile", None), P("tile", None), P(), P(), P(), P(), P())
    return jax.shard_map(
        local, mesh=mesh, in_specs=placed, out_specs=P("wave", "tile", None), check_vma=False
    )
```

```python
import jax
import jax.numpy as jnp
from jax import lax
from jax.experimental import pallas as pl
from jax.experimental.pallas import tpu as pltpu
from jax.sharding import PartitionSpec as P

ITERS = 8
LOWER = 0.1
UPPER = 2.0
THETA = (UPPER + LOWER) / 2.0
DELTA = (UPPER - LOWER) / 2.0
SIGMA_ONE = THETA / DELTA
CURRENT = 2.0

TAU = [1.0, SIGMA_ONE]
for _ in range(ITERS):
    TAU.append(2.0 * SIGMA_ONE * TAU[-1] - TAU[-2])
OMEGA = 2.0 * (THETA - 1.0) / DELTA

LANES = 128
SUBS = 8
PARTS = 8
ROWS = 32
HALO = 8
HELD = ROWS + 2 * HALO
SPAN = 64
FIRST = 8
CORE = FIRST + HALO
LAST = FIRST + HELD
UNROLL = ((8, 6), (9, 5), (11, 4), (7, 6), (8, 5), (8, 5), (7, 5), (11, 3))
MESH = pl.DeviceIdType.MESH
F32 = jnp.float32
BF16 = jnp.bfloat16


def chosen(index, table):
    value = jnp.float32(0.0)
    for position, entry in enumerate(table):
        value = jnp.where(index == position, jnp.float32(entry), value)
    return value


def slot_column(pair, half, wave_pos):
    middle = jnp.logical_or(pair == 1, pair == 2)
    ahead = jnp.where(pair == 0, 2, jnp.where(middle, 1 + 2 * half, 0))
    offset = jnp.where(middle, pair - 1, half)
    return 2 * lax.rem(wave_pos + ahead, 4) + offset


def thirds(values):
    high = values.astype(BF16)
    rest = values - high.astype(F32)
    middle = rest.astype(BF16)
    low = (rest - middle.astype(F32)).astype(BF16)
    return high, middle, low


def kernel(
    fields_in, sigma_in, wavenumbers_in, weights_in, counts_in, electrodes_in, pairs_in, out,
    fields, sigma, wavenumbers, weights, counts, electrodes, pairs,
    into, back, weave, stage, sig_n, sig_s, sig, diag, face_n, face_w,
    an, aw, root, close, vectors, src, w, acc, from_low, from_high,
    in_sem, h_send, h_recv, s_send, s_recv, r_send, r_recv,
):
    per_group = fields.shape[0]
    tile_count = lax.axis_size("tile")
    wave_count = lax.axis_size("wave")
    tile_pos = lax.axis_index("tile")
    wave_pos = lax.axis_index("wave")
    south = {"tile": lax.rem(tile_pos + 1, tile_count)}
    north = {"tile": lax.rem(tile_pos + tile_count - 1, tile_count)}
    above = {"wave": lax.rem(wave_pos + 1, wave_count)}
    below = {"wave": lax.rem(wave_pos + wave_count - 1, wave_count)}

    barrier = pltpu.get_barrier_semaphore()
    for other in (south, north, above, below):
        pl.semaphore_signal(barrier, inc=1, device_id=other, device_id_type=MESH)

    loads = [
        pltpu.make_async_copy(source, target, in_sem.at[place])
        for place, (source, target) in enumerate((
            (fields_in, fields), (sigma_in, sigma), (wavenumbers_in, wavenumbers), (weights_in, weights),
            (counts_in, counts), (electrodes_in, electrodes), (pairs_in, pairs)))
    ]
    for load in loads:
        load.start()

    lane = lax.broadcasted_iota(jnp.int32, (SUBS, LANES), 1)
    sub = lax.broadcasted_iota(jnp.int32, (SUBS, LANES), 0)
    first_lane = lane == 0
    last_lane = lane == LANES - 1
    zero = jnp.zeros((SUBS, LANES), F32)

    @pl.loop(0, PARTS)
    def _(block):
        wide = PARTS * LANES
        base = pl.multiple_of(block * LANES, LANES)
        row = lax.broadcasted_iota(jnp.int32, (LANES, wide), 0) + base
        column = lax.broadcasted_iota(jnp.int32, (LANES, wide), 1)
        into[pl.ds(base, LANES), :] = jnp.where(
            row == lax.rem(column, LANES) * PARTS + lax.div(column, LANES), 1.0, 0.0).astype(BF16)
        back[pl.ds(base, LANES), :] = jnp.where(
            column == lax.rem(row, LANES) * PARTS + lax.div(row, LANES), 1.0, 0.0).astype(BF16)

    row = lax.broadcasted_iota(jnp.int32, weave.shape, 0)
    column = lax.broadcasted_iota(jnp.int32, weave.shape, 1)
    weave[...] = jnp.where(
        column == lax.rem(row, SUBS) * ROWS + lax.div(row, SUBS), 1.0, 0.0).astype(BF16)

    for part in range(PARTS):
        rows8 = pl.ds(part * SUBS, SUBS)
        for row in range(LAST, SPAN):
            an[row, rows8, :] = zero
            aw[row, rows8, :] = zero
            src[0, row] = zero
            for buf in range(2):
                w[buf, row, rows8, :] = zero
        for edge in (0, LAST):
            sig[part, pl.ds(edge, FIRST), :] = zero + 1.0

    for load in loads:
        load.wait()
    pl.semaphore_wait(barrier, 4)

    def remote(source, target, send, recv, device):
        return pltpu.make_async_remote_copy(
            src_ref=source, dst_ref=target, send_sem=send, recv_sem=recv,
            device_id=device, device_id_type=MESH,
        )

    sig_south = remote(sigma.at[pl.ds(ROWS - HALO, HALO)], sig_n, s_send.at[0], s_recv.at[0], south)
    sig_north = remote(sigma.at[pl.ds(0, HALO)], sig_s, s_send.at[1], s_recv.at[1], north)
    sig_south.start()
    sig_north.start()

    def halo_copies(pair):
        return (
            remote(stage.at[pair, pl.ds(ROWS, HALO)], stage.at[pair, pl.ds(0, HALO)],
                   h_send.at[0, pair], h_recv.at[0, pair], south),
            remote(stage.at[pair, pl.ds(HALO, HALO)], stage.at[pair, pl.ds(HALO + ROWS, HALO)],
                   h_send.at[1, pair], h_recv.at[1, pair], north),
        )

    @pl.loop(0, 4)
    def _(pair):
        columns = [slot_column(pair, half, wave_pos) for half in range(2)]
        block = jnp.concatenate(
            [fields[k, columns[half]] for half in range(2) for k in range(per_group)], axis=0)
        woven = jnp.dot(weave[...], block, preferred_element_type=F32).astype(BF16)
        moved = jnp.dot(woven, into[...], preferred_element_type=F32)
        for row in range(ROWS):
            for part in range(PARTS):
                stage[pair, HALO + row, pl.ds(part * SUBS, SUBS), :] = moved[
                    row * SUBS:(row + 1) * SUBS, part * LANES:(part + 1) * LANES]
        for copy in halo_copies(pair):
            copy.start()

    def by_wavenumber(scalars):
        value = zero
        for k, scalar in enumerate(scalars):
            value = jnp.where(lax.rem(sub, per_group) == k, scalar, value)
        return value

    group = [wave_pos * per_group + k for k in range(per_group)]
    square = by_wavenumber([wavenumbers[g] * wavenumbers[g] for g in group])
    final = by_wavenumber([
        weights[g] * chosen(counts[g], [1.0 / tau for tau in TAU[: ITERS + 1]]) for g in group])
    for step in range(ITERS):
        live = [step - (ITERS - counts[g]) for g in group]
        vectors[3 * step] = by_wavenumber([
            jnp.where(at < 0, F32(2.0), jnp.where(at == 0, F32(1.0 + 0.5 * OMEGA), F32(OMEGA))) for at in live])
        vectors[3 * step + 1] = by_wavenumber([
            jnp.where(at < 0, F32(0.0), jnp.where(at == 0, F32(0.5), F32(1.0))) for at in live])
        vectors[3 * step + 2] = by_wavenumber([chosen(at, [0.5] + TAU[1:ITERS]) for at in live])

    sig_south.wait_recv()
    sig_north.wait_recv()
    whole = jnp.concatenate([sig_n[...], sigma[...], sig_s[...]], axis=0)
    moved = jnp.dot(jnp.concatenate(thirds(whole), axis=0), into[...], preferred_element_type=F32)
    moved = (moved[:HELD] + moved[HELD:2 * HELD]) + moved[2 * HELD:]
    for part in range(PARTS):
        sig[part, pl.ds(FIRST, HELD), :] = moved[:, part * LANES:(part + 1) * LANES]

    @pl.loop(1, LAST // SUBS)
    def _(row_tile):
        row = pl.multiple_of(row_tile * SUBS, SUBS)
        place = tile_pos * ROWS + row - CORE + sub
        last_row = tile_count * ROWS
        centre = [sig[part, pl.ds(row, SUBS), :] for part in range(PARTS)]
        for part in range(PARTS):
            mid = centre[part]
            up = jnp.where(place == 0, 0.0, sig[part, pl.ds(row - 1, SUBS), :])
            down = jnp.where(place == last_row - 1, 0.0, sig[part, pl.ds(row + 1, SUBS), :])
            if part == 0:
                left = jnp.where(first_lane, 0.0, pltpu.roll(centre[-1], 1, 1))
            else:
                left = centre[part - 1]
            if part == PARTS - 1:
                right = jnp.where(last_lane, 0.0, pltpu.roll(centre[0], LANES - 1, 1))
            else:
                right = centre[part + 1]
            faces = [0.5 * (mid + near) for near in (up, down, left, right)]
            diag[part, pl.ds(row, SUBS), :] = (faces[0] + faces[1]) + (faces[2] + faces[3])
            outside = jnp.logical_or(place == 0, place == last_row)
            face_n[part, pl.ds(row, SUBS), :] = jnp.where(outside, 0.0, (2.0 / DELTA) * faces[0])
            west = (2.0 / DELTA) * faces[2]
            if part == 0:
                west = jnp.where(first_lane, 0.0, west)
            face_w[part, pl.ds(row, SUBS), :] = west

    def couplings(row, above_row):
        def spread(ref, part):
            return jnp.broadcast_to(ref[part, pl.ds(row, 1), :], (SUBS, LANES))

        here = []
        for part in range(PARTS):
            rows8 = pl.ds(part * SUBS, SUBS)
            value = spread(diag, part) + square * spread(sig, part)
            guess = lax.rsqrt(value)
            guess = guess * (1.5 - (0.5 * value) * (guess * guess))
            root[row, rows8, :] = value * guess
            close[row, rows8, :] = final * guess
            an[row, rows8, :] = spread(face_n, part) * (guess * above_row[part])
            here.append(guess)
        src[1, row] = here[0]
        for part in range(PARTS):
            beside = here[part - 1] if part else pltpu.roll(here[-1], 1, 1)
            aw[row, pl.ds(part * SUBS, SUBS), :] = spread(face_w, part) * (here[part] * beside)
        return tuple(here)

    lax.fori_loop(FIRST, LAST, couplings, (zero,) * PARTS)

    def sweep(step):
        now, later = step % 2, (step + 1) % 2
        before = now if step == 0 else later
        centre_gain = vectors[3 * step]
        side_gain = vectors[3 * step + 1]
        charge = vectors[3 * step + 2]
        start = FIRST + step + 1
        unroll, blocks = UNROLL[step]
        parts = [pl.ds(part * SUBS, SUBS) for part in range(PARTS)]

        def one(row, carry):
            old, sums = carry
            edge = pltpu.roll(w[now, row, parts[-1], :], 1, 1)
            u, held, flow_first = [], [], None
            for part, at in enumerate(parts):
                here = w[now, row, at, :]
                north_c = an[row, at, :]
                value = side_gain * (sums[part] + north_c * here) + (
                    centre_gain * old[part] - w[before, row - 1, at, :])
                if part == 0:
                    value = value + charge * src[0, row - 1]
                w[later, row - 1, at, :] = value
                west_c = aw[row, at, :]
                flow = west_c * here
                if part == 0:
                    flow_first = pltpu.roll(flow, LANES - 1, 1)
                else:
                    held[-1] = held[-1] + flow
                held.append(north_c * old[part] + west_c * (u[-1] if part else edge))
                u.append(here)
            held[-1] = held[-1] + flow_first
            return tuple(u), tuple(held)

        def body(block, carry):
            for place in range(unroll):
                carry = one(start + unroll * block + place, carry)
            return carry

        opening = tuple(w[now, start - 1, at, :] for at in parts)
        lax.fori_loop(0, blocks, body, (opening, (zero,) * PARTS))

    def rs_copies(pair):
        slot = 2 * pair
        return (
            remote(acc.at[slot], from_low.at[pair], r_send.at[0, pair], r_recv.at[0, pair], above),
            remote(acc.at[slot + 1], from_high.at[pair], r_send.at[1, pair], r_recv.at[1, pair], below),
        )

    @pl.loop(0, 4)
    def _(pair):
        columns = [slot_column(pair, half, wave_pos) for half in range(2)]
        spots = []
        for end in range(2):
            low, high = [electrodes[pairs[end, column]] for column in columns]
            spots.append(jnp.where(sub < per_group, low, high) - tile_pos * ROWS + CORE)
        for copy in halo_copies(pair):
            copy.wait_recv()

        @pl.loop(FIRST, LAST)
        def _(row):
            for part in range(PARTS):
                rows8 = pl.ds(part * SUBS, SUBS)
                w[0, row, rows8, :] = stage[pair, row - FIRST, rows8, :] * root[row, rows8, :]
            spot = jnp.where(row == spots[0], CURRENT, 0.0) - jnp.where(row == spots[1], CURRENT, 0.0)
            spot = (2.0 / DELTA) * spot * src[1, row]
            src[0, row] = jnp.where(first_lane, spot, 0.0)

        for step in range(ITERS):
            sweep(step)

        @pl.loop(0, ROWS)
        def _(row):
            for part in range(PARTS):
                rows8 = pl.ds(part * SUBS, SUBS)
                value = close[CORE + row, rows8, :] * w[ITERS % 2, CORE + row, rows8, :]
                value = value + pltpu.roll(value, SUBS - 2, 0)
                value = value + pltpu.roll(value, SUBS - 1, 0)
                for half in range(2):
                    acc[2 * pair + half, part, pl.ds(row, 1), :] = value[half * per_group:half * per_group + 1]

        @pl.when(pair == 1)
        def _():
            rs_copies(0)[0].wait_recv()
            acc[2] += from_low[0]

        @pl.when(pair == 2)
        def _():
            rs_copies(0)[1].wait_recv()
            acc[5] += from_high[0]

        @pl.when(pair < 3)
        def _():
            for copy in rs_copies(pair):
                copy.start()

    for pair in (1, 2):
        for copy in rs_copies(pair):
            copy.wait_recv()
    total = jnp.concatenate([
        jnp.concatenate([acc[6 + half, part] + (from_low[1 + half, part] + from_high[1 + half, part])
                         for part in range(PARTS)], axis=1)
        for half in range(2)], axis=0)
    moved = jnp.dot(jnp.concatenate(thirds(total), axis=0), back[...], preferred_element_type=F32)
    for half in range(2):
        cut = half * ROWS
        out[half] = (moved[cut:cut + ROWS] + moved[2 * ROWS + cut:3 * ROWS + cut]) + moved[
            4 * ROWS + cut:5 * ROWS + cut]

    for pair in range(3):
        for copy in rs_copies(pair):
            copy.wait_send()
    for pair in range(4):
        for copy in halo_copies(pair):
            copy.wait_send()
    sig_south.wait_send()
    sig_north.wait_send()


def local(*arrays):
    arrays = (*arrays[:-1], arrays[-1].T)
    fields = arrays[0]
    per_group, sources, rows, depth = fields.shape
    small = [pltpu.SMEM(a.shape, a.dtype) for a in arrays[2:]]
    tall = pltpu.VMEM((SPAN, PARTS * SUBS, LANES), F32)
    flat = pltpu.VMEM((PARTS, SPAN, LANES), F32)
    return pl.pallas_call(
        kernel,
        out_shape=jax.ShapeDtypeStruct((sources // 4, rows, depth), F32),
        in_specs=[pl.BlockSpec(memory_space=pltpu.HBM)] * len(arrays),
        out_specs=pl.BlockSpec(memory_space=pltpu.VMEM),
        scratch_shapes=[
            pltpu.VMEM(fields.shape, fields.dtype),
            pltpu.VMEM((rows, depth), F32),
            *small,
            pltpu.VMEM((depth, depth), BF16),
            pltpu.VMEM((depth, depth), BF16),
            pltpu.VMEM((SUBS * rows, SUBS * rows), BF16),
            pltpu.VMEM((4, HELD, PARTS * SUBS, LANES), F32),
            pltpu.VMEM((HALO, depth), F32),
            pltpu.VMEM((HALO, depth), F32),
            flat, flat, flat, flat,
            tall, tall, tall, tall,
            pltpu.VMEM((3 * ITERS, SUBS, LANES), F32),
            pltpu.VMEM((2, SPAN, SUBS, LANES), F32),
            pltpu.VMEM((2, SPAN, PARTS * SUBS, LANES), F32),
            pltpu.VMEM((sources, PARTS, rows, LANES), F32),
            pltpu.VMEM((3, PARTS, rows, LANES), F32),
            pltpu.VMEM((3, PARTS, rows, LANES), F32),
            pltpu.SemaphoreType.DMA((7,)),
            pltpu.SemaphoreType.DMA((2, 4)),
            pltpu.SemaphoreType.DMA((2, 4)),
            pltpu.SemaphoreType.DMA((2,)),
            pltpu.SemaphoreType.DMA((2,)),
            pltpu.SemaphoreType.DMA((2, 3)),
            pltpu.SemaphoreType.DMA((2, 3)),
        ],
        compiler_params=pltpu.CompilerParams(
            collective_id=0, has_side_effects=True, vmem_limit_bytes=63 * 1024 * 1024),
    )(*arrays)


def solution(mesh):
    placed = (P("wave", None, "tile", None), P("tile", None), P(), P(), P(), P(), P())
    return jax.shard_map(
        local, mesh=mesh, in_specs=placed, out_specs=P("wave", "tile", None), check_vma=False
    )
```

```python
import jax
import jax.numpy as jnp
from jax import lax
from jax.experimental import pallas as pl
from jax.experimental.pallas import tpu as pltpu
from jax.sharding import PartitionSpec as P

ITERS = 8
LOWER = 0.1
UPPER = 2.0
THETA = (UPPER + LOWER) / 2.0
DELTA = (UPPER - LOWER) / 2.0
SIGMA_ONE = THETA / DELTA
CURRENT = 2.0

TAU = [1.0, SIGMA_ONE]
for _ in range(ITERS):
    TAU.append(2.0 * SIGMA_ONE * TAU[-1] - TAU[-2])
OMEGA = 2.0 * (THETA - 1.0) / DELTA

LANES = 128
SUBS = 8
PARTS = 8
ROWS = 32
HALO = 8
HELD = ROWS + 2 * HALO
SPAN = 64
FIRST = 8
CORE = FIRST + HALO
LAST = FIRST + HELD
UNROLL = ((8, 6), (9, 5), (11, 4), (7, 6), (8, 5), (8, 5), (7, 5), (11, 3))
MESH = pl.DeviceIdType.MESH
F32 = jnp.float32
BF16 = jnp.bfloat16


def chosen(index, table):
    value = jnp.float32(0.0)
    for position, entry in enumerate(table):
        value = jnp.where(index == position, jnp.float32(entry), value)
    return value


def slot_column(pair, half, wave_pos):
    middle = jnp.logical_or(pair == 1, pair == 2)
    ahead = jnp.where(pair == 0, 2, jnp.where(middle, 1 + 2 * half, 0))
    offset = jnp.where(middle, pair - 1, half)
    return 2 * lax.rem(wave_pos + ahead, 4) + offset


def thirds(values):
    high = values.astype(BF16)
    rest = values - high.astype(F32)
    middle = rest.astype(BF16)
    low = (rest - middle.astype(F32)).astype(BF16)
    return high, middle, low


def kernel(
    fields_in, sigma_in, wavenumbers_in, weights_in, counts_in, electrodes_in, pairs_in, out,
    fields, sigma, wavenumbers, weights, counts, electrodes, pairs,
    into, back, weave, stage, sig_n, sig_s, sig, diag, face_n, face_w,
    an, aw, root, close, vectors, src, w, acc, from_low, from_high,
    in_sem, h_send, h_recv, s_send, s_recv, r_send, r_recv,
):
    per_group = fields.shape[0]
    tile_count = lax.axis_size("tile")
    wave_count = lax.axis_size("wave")
    tile_pos = lax.axis_index("tile")
    wave_pos = lax.axis_index("wave")
    south = {"tile": lax.rem(tile_pos + 1, tile_count)}
    north = {"tile": lax.rem(tile_pos + tile_count - 1, tile_count)}
    above = {"wave": lax.rem(wave_pos + 1, wave_count)}
    below = {"wave": lax.rem(wave_pos + wave_count - 1, wave_count)}

    barrier = pltpu.get_barrier_semaphore()
    for other in (south, north, above, below):
        pl.semaphore_signal(barrier, inc=1, device_id=other, device_id_type=MESH)

    loads = [
        pltpu.make_async_copy(source, target, in_sem.at[place])
        for place, (source, target) in enumerate((
            (fields_in, fields), (sigma_in, sigma), (wavenumbers_in, wavenumbers), (weights_in, weights),
            (counts_in, counts), (electrodes_in, electrodes), (pairs_in, pairs)))
    ]
    for load in loads:
        load.start()

    lane = lax.broadcasted_iota(jnp.int32, (SUBS, LANES), 1)
    sub = lax.broadcasted_iota(jnp.int32, (SUBS, LANES), 0)
    first_lane = lane == 0
    last_lane = lane == LANES - 1
    zero = jnp.zeros((SUBS, LANES), F32)

    @pl.loop(0, PARTS)
    def _(block):
        wide = PARTS * LANES
        base = pl.multiple_of(block * LANES, LANES)
        row = lax.broadcasted_iota(jnp.int32, (LANES, wide), 0) + base
        column = lax.broadcasted_iota(jnp.int32, (LANES, wide), 1)
        into[pl.ds(base, LANES), :] = jnp.where(
            row == lax.rem(column, LANES) * PARTS + lax.div(column, LANES), 1.0, 0.0).astype(BF16)
        back[pl.ds(base, LANES), :] = jnp.where(
            column == lax.rem(row, LANES) * PARTS + lax.div(row, LANES), 1.0, 0.0).astype(BF16)

    row = lax.broadcasted_iota(jnp.int32, weave.shape, 0)
    column = lax.broadcasted_iota(jnp.int32, weave.shape, 1)
    weave[...] = jnp.where(
        column == lax.rem(row, SUBS) * ROWS + lax.div(row, SUBS), 1.0, 0.0).astype(BF16)

    for part in range(PARTS):
        rows8 = pl.ds(part * SUBS, SUBS)
        for row in range(LAST, SPAN):
            an[row, rows8, :] = zero
            aw[row, rows8, :] = zero
            src[0, row] = zero
            for buf in range(2):
                w[buf, row, rows8, :] = zero
        for edge in (0, LAST):
            sig[part, pl.ds(edge, FIRST), :] = zero + 1.0

    for load in loads:
        load.wait()
    pl.semaphore_wait(barrier, 4)

    def remote(source, target, send, recv, device):
        return pltpu.make_async_remote_copy(
            src_ref=source, dst_ref=target, send_sem=send, recv_sem=recv,
            device_id=device, device_id_type=MESH,
        )

    sig_south = remote(sigma.at[pl.ds(ROWS - HALO, HALO)], sig_n, s_send.at[0], s_recv.at[0], south)
    sig_north = remote(sigma.at[pl.ds(0, HALO)], sig_s, s_send.at[1], s_recv.at[1], north)
    sig_south.start()
    sig_north.start()

    def halo_copies(pair):
        return (
            remote(stage.at[pair, pl.ds(ROWS * SUBS, HALO * SUBS)], stage.at[pair, pl.ds(0, HALO * SUBS)],
                   h_send.at[0, pair], h_recv.at[0, pair], south),
            remote(stage.at[pair, pl.ds(HALO * SUBS, HALO * SUBS)],
                   stage.at[pair, pl.ds((HALO + ROWS) * SUBS, HALO * SUBS)],
                   h_send.at[1, pair], h_recv.at[1, pair], north),
        )

    @pl.loop(0, 2)
    def _(batch):
        woven = []
        for pair in (2 * batch, 2 * batch + 1):
            columns = [slot_column(pair, half, wave_pos) for half in range(2)]
            block = jnp.concatenate(
                [fields[k, columns[half]] for half in range(2) for k in range(per_group)], axis=0)
            woven.append(jnp.dot(weave[...], block, preferred_element_type=F32).astype(BF16))
        moved = jnp.dot(jnp.concatenate(woven, axis=0), into[...], preferred_element_type=F32).astype(BF16)
        for place, pair in enumerate((2 * batch, 2 * batch + 1)):
            stage[pair, pl.ds(HALO * SUBS, ROWS * SUBS), :] = moved[place * ROWS * SUBS:(place + 1) * ROWS * SUBS]
            for copy in halo_copies(pair):
                copy.start()

    def by_wavenumber(scalars):
        value = zero
        for k, scalar in enumerate(scalars):
            value = jnp.where(lax.rem(sub, per_group) == k, scalar, value)
        return value

    def everywhere(scalars):
        return jnp.concatenate([by_wavenumber(scalars)] * PARTS, axis=0)

    group = [wave_pos * per_group + k for k in range(per_group)]
    square = by_wavenumber([wavenumbers[g] * wavenumbers[g] for g in group])
    final = by_wavenumber([
        weights[g] * chosen(counts[g], [1.0 / tau for tau in TAU[: ITERS + 1]]) for g in group])
    for step in range(ITERS):
        live = [step - (ITERS - counts[g]) for g in group]
        vectors[3 * step] = everywhere([
            jnp.where(at < 0, F32(2.0), jnp.where(at == 0, F32(1.0 + 0.5 * OMEGA), F32(OMEGA))) for at in live])
        vectors[3 * step + 1] = everywhere([
            jnp.where(at < 0, F32(0.0), jnp.where(at == 0, F32(0.5), F32(1.0))) for at in live])
        vectors[3 * step + 2] = everywhere([chosen(at, [0.5] + TAU[1:ITERS]) for at in live])

    sig_south.wait_recv()
    sig_north.wait_recv()
    whole = jnp.concatenate([sig_n[...], sigma[...], sig_s[...]], axis=0)
    moved = jnp.dot(jnp.concatenate(thirds(whole), axis=0), into[...], preferred_element_type=F32)
    moved = (moved[:HELD] + moved[HELD:2 * HELD]) + moved[2 * HELD:]
    for part in range(PARTS):
        sig[part, pl.ds(FIRST, HELD), :] = moved[:, part * LANES:(part + 1) * LANES]

    @pl.loop(1, LAST // SUBS)
    def _(row_tile):
        row = pl.multiple_of(row_tile * SUBS, SUBS)
        place = tile_pos * ROWS + row - CORE + sub
        last_row = tile_count * ROWS
        centre = [sig[part, pl.ds(row, SUBS), :] for part in range(PARTS)]
        for part in range(PARTS):
            mid = centre[part]
            up = jnp.where(place == 0, 0.0, sig[part, pl.ds(row - 1, SUBS), :])
            down = jnp.where(place == last_row - 1, 0.0, sig[part, pl.ds(row + 1, SUBS), :])
            if part == 0:
                left = jnp.where(first_lane, 0.0, pltpu.roll(centre[-1], 1, 1))
            else:
                left = centre[part - 1]
            if part == PARTS - 1:
                right = jnp.where(last_lane, 0.0, pltpu.roll(centre[0], LANES - 1, 1))
            else:
                right = centre[part + 1]
            faces = [0.5 * (mid + near) for near in (up, down, left, right)]
            diag[part, pl.ds(row, SUBS), :] = (faces[0] + faces[1]) + (faces[2] + faces[3])
            outside = jnp.logical_or(place == 0, place == last_row)
            face_n[part, pl.ds(row, SUBS), :] = jnp.where(outside, 0.0, (2.0 / DELTA) * faces[0])
            west = (2.0 / DELTA) * faces[2]
            if part == 0:
                west = jnp.where(first_lane, 0.0, west)
            face_w[part, pl.ds(row, SUBS), :] = west

    def couplings(row, above_row):
        def spread(ref, part):
            return jnp.broadcast_to(ref[part, pl.ds(row, 1), :], (SUBS, LANES))

        here = []
        for part in range(PARTS):
            rows8 = pl.ds(part * SUBS, SUBS)
            value = spread(diag, part) + square * spread(sig, part)
            guess = lax.rsqrt(value)
            guess = guess * (1.5 - (0.5 * value) * (guess * guess))
            root[row, rows8, :] = value * guess
            close[row, rows8, :] = final * guess
            an[row, rows8, :] = spread(face_n, part) * (guess * above_row[part])
            here.append(guess)
        src[1, row] = here[0]
        for part in range(PARTS):
            beside = here[part - 1] if part else pltpu.roll(here[-1], 1, 1)
            aw[row, pl.ds(part * SUBS, SUBS), :] = spread(face_w, part) * (here[part] * beside)
        return tuple(here)

    def two_rows(block, above_row):
        return couplings(FIRST + 2 * block + 1, couplings(FIRST + 2 * block, above_row))

    lax.fori_loop(0, HELD // 2, two_rows, (zero,) * PARTS)

    def sweep(step):
        now, later = step % 2, (step + 1) % 2
        before = now if step == 0 else later
        charge = vectors[3 * step + 2, pl.ds(0, SUBS), :]
        start = FIRST + step + 1
        unroll, blocks = UNROLL[step]
        parts = [pl.ds(part * SUBS, SUBS) for part in range(PARTS)]

        def one(row, carry):
            old, sums = carry
            edge = pltpu.roll(w[now, row, parts[-1], :], 1, 1)
            u, held, flow_first = [], [], None
            for part, at in enumerate(parts):
                here = w[now, row, at, :]
                north_c = an[row, at, :]
                side_gain, centre_gain = vectors[3 * step + 1, at, :], vectors[3 * step, at, :]
                value = side_gain * (sums[part] + north_c * here) + (
                    centre_gain * old[part] - w[before, row - 1, at, :])
                if part == 0:
                    value = value + charge * src[0, row - 1]
                w[later, row - 1, at, :] = value
                west_c = aw[row, at, :]
                flow = west_c * here
                if part == 0:
                    flow_first = pltpu.roll(flow, LANES - 1, 1)
                else:
                    held[-1] = held[-1] + flow
                held.append(north_c * old[part] + west_c * (u[-1] if part else edge))
                u.append(here)
            held[-1] = held[-1] + flow_first
            return tuple(u), tuple(held)

        def body(block, carry):
            for place in range(unroll):
                carry = one(start + unroll * block + place, carry)
            return carry

        opening = tuple(w[now, start - 1, at, :] for at in parts)
        lax.fori_loop(0, blocks, body, (opening, (zero,) * PARTS))

    def rs_copies(pair):
        slot = 2 * pair
        return (
            remote(acc.at[slot], from_low.at[pair], r_send.at[0, pair], r_recv.at[0, pair], above),
            remote(acc.at[slot + 1], from_high.at[pair], r_send.at[1, pair], r_recv.at[1, pair], below),
        )

    @pl.loop(0, 4)
    def _(pair):
        columns = [slot_column(pair, half, wave_pos) for half in range(2)]
        spots = []
        for end in range(2):
            low, high = [electrodes[pairs[end, column]] for column in columns]
            spots.append(jnp.where(sub < per_group, low, high) - tile_pos * ROWS + CORE)
        for copy in halo_copies(pair):
            copy.wait_recv()

        @pl.loop(0, HELD // 4)
        def _(block):
            for twin in (2 * block, 2 * block + 1):
                for part in range(PARTS):
                    rows8 = pl.ds(part * SUBS, SUBS)
                    given = stage[pair, pl.ds(twin * 2 * SUBS, 2 * SUBS), pl.ds(part * LANES, LANES)].astype(F32)
                    for place in range(2):
                        row = FIRST + 2 * twin + place
                        w[0, row, rows8, :] = given[place * SUBS:(place + 1) * SUBS] * root[row, rows8, :]
            for place in range(4):
                row = FIRST + 4 * block + place
                spot = jnp.where(row == spots[0], CURRENT, 0.0) - jnp.where(row == spots[1], CURRENT, 0.0)
                spot = (2.0 / DELTA) * spot * src[1, row]
                src[0, row] = jnp.where(first_lane, spot, 0.0)

        for step in range(ITERS):
            sweep(step)

        @pl.loop(0, ROWS // 4)
        def _(block):
            for row in [4 * block + place for place in range(4)]:
                for part in range(PARTS):
                    rows8 = pl.ds(part * SUBS, SUBS)
                    value = close[CORE + row, rows8, :] * w[ITERS % 2, CORE + row, rows8, :]
                    value = value + pltpu.roll(value, SUBS - 2, 0)
                    value = value + pltpu.roll(value, SUBS - 1, 0)
                    for half in range(2):
                        acc[2 * pair + half, part, pl.ds(row, 1), :] = value[half * per_group:half * per_group + 1]

        @pl.when(pair == 1)
        def _():
            rs_copies(0)[0].wait_recv()
            acc[2] += from_low[0]

        @pl.when(pair == 2)
        def _():
            rs_copies(0)[1].wait_recv()
            acc[5] += from_high[0]

        @pl.when(pair < 3)
        def _():
            for copy in rs_copies(pair):
                copy.start()

    for pair in (1, 2):
        for copy in rs_copies(pair):
            copy.wait_recv()
    total = jnp.concatenate([
        jnp.concatenate([acc[6 + half, part] + (from_low[1 + half, part] + from_high[1 + half, part])
                         for part in range(PARTS)], axis=1)
        for half in range(2)], axis=0)
    moved = jnp.dot(jnp.concatenate(thirds(total), axis=0), back[...], preferred_element_type=F32)
    for half in range(2):
        cut = half * ROWS
        out[half] = (moved[cut:cut + ROWS] + moved[2 * ROWS + cut:3 * ROWS + cut]) + moved[
            4 * ROWS + cut:5 * ROWS + cut]

    for pair in range(3):
        for copy in rs_copies(pair):
            copy.wait_send()
    for pair in range(4):
        for copy in halo_copies(pair):
            copy.wait_send()
    sig_south.wait_send()
    sig_north.wait_send()


def local(*arrays):
    arrays = (*arrays[:-1], arrays[-1].T)
    fields = arrays[0]
    per_group, sources, rows, depth = fields.shape
    small = [pltpu.SMEM(a.shape, a.dtype) for a in arrays[2:]]
    tall = pltpu.VMEM((SPAN, PARTS * SUBS, LANES), F32)
    flat = pltpu.VMEM((PARTS, SPAN, LANES), F32)
    return pl.pallas_call(
        kernel,
        out_shape=jax.ShapeDtypeStruct((sources // 4, rows, depth), F32),
        in_specs=[pl.BlockSpec(memory_space=pltpu.HBM)] * len(arrays),
        out_specs=pl.BlockSpec(memory_space=pltpu.VMEM),
        scratch_shapes=[
            pltpu.VMEM(fields.shape, fields.dtype),
            pltpu.VMEM((rows, depth), F32),
            *small,
            pltpu.VMEM((depth, depth), BF16),
            pltpu.VMEM((depth, depth), BF16),
            pltpu.VMEM((SUBS * rows, SUBS * rows), BF16),
            pltpu.VMEM((4, HELD * SUBS, depth), BF16),
            pltpu.VMEM((HALO, depth), F32),
            pltpu.VMEM((HALO, depth), F32),
            flat, flat, flat, flat,
            tall, tall, tall, tall,
            pltpu.VMEM((3 * ITERS, PARTS * SUBS, LANES), F32),
            pltpu.VMEM((2, SPAN, SUBS, LANES), F32),
            pltpu.VMEM((2, SPAN, PARTS * SUBS, LANES), F32),
            pltpu.VMEM((sources, PARTS, rows, LANES), F32),
            pltpu.VMEM((3, PARTS, rows, LANES), F32),
            pltpu.VMEM((3, PARTS, rows, LANES), F32),
            pltpu.SemaphoreType.DMA((7,)),
            pltpu.SemaphoreType.DMA((2, 4)),
            pltpu.SemaphoreType.DMA((2, 4)),
            pltpu.SemaphoreType.DMA((2,)),
            pltpu.SemaphoreType.DMA((2,)),
            pltpu.SemaphoreType.DMA((2, 3)),
            pltpu.SemaphoreType.DMA((2, 3)),
        ],
        compiler_params=pltpu.CompilerParams(
            collective_id=0, has_side_effects=True, vmem_limit_bytes=63 * 1024 * 1024),
    )(*arrays)


def solution(mesh):
    placed = (P("wave", None, "tile", None), P("tile", None), P(), P(), P(), P(), P())
    return jax.shard_map(
        local, mesh=mesh, in_specs=placed, out_specs=P("wave", "tile", None), check_vma=False
    )
```

```python
import jax
import jax.numpy as jnp
from jax import lax
from jax.experimental import pallas as pl
from jax.experimental.pallas import tpu as pltpu
from jax.sharding import PartitionSpec as P

ITERS = 8
LOWER = 0.1
UPPER = 2.0
THETA = (UPPER + LOWER) / 2.0
DELTA = (UPPER - LOWER) / 2.0
SIGMA_ONE = THETA / DELTA
CURRENT = 2.0

TAU = [1.0, SIGMA_ONE]
for _ in range(ITERS):
    TAU.append(2.0 * SIGMA_ONE * TAU[-1] - TAU[-2])
OMEGA = 2.0 * (THETA - 1.0) / DELTA

LANES = 128
SUBS = 8
PARTS = 8
ROWS = 32
HALO = 8
HELD = ROWS + 2 * HALO
SPAN = 64
FIRST = 8
CORE = FIRST + HALO
LAST = FIRST + HELD
UNROLL = ((8, 6), (9, 5), (11, 4), (7, 6), (8, 5), (8, 5), (7, 5), (11, 3))
MESH = pl.DeviceIdType.MESH
F32 = jnp.float32
BF16 = jnp.bfloat16


def chosen(index, table):
    value = jnp.float32(0.0)
    for position, entry in enumerate(table):
        value = jnp.where(index == position, jnp.float32(entry), value)
    return value


def slot_column(pair, half, wave_pos):
    middle = jnp.logical_or(pair == 1, pair == 2)
    ahead = jnp.where(pair == 0, 2, jnp.where(middle, 1 + 2 * half, 0))
    offset = jnp.where(middle, pair - 1, half)
    return 2 * lax.rem(wave_pos + ahead, 4) + offset


def thirds(values):
    high = values.astype(BF16)
    rest = values - high.astype(F32)
    middle = rest.astype(BF16)
    low = (rest - middle.astype(F32)).astype(BF16)
    return high, middle, low


def kernel(
    fields_in, sigma_in, wavenumbers_in, weights_in, counts_in, electrodes_in, pairs_in, out,
    fields, sigma, wavenumbers, weights, counts, electrodes, pairs,
    into, back, weave, stage, sig_n, sig_s, sig, diag, face_n, face_w,
    an, aw, root, close, vectors, src, w, acc, from_low, from_high,
    in_sem, h_send, h_recv, s_send, s_recv, r_send, r_recv,
):
    per_group = fields.shape[0]
    tile_count = lax.axis_size("tile")
    wave_count = lax.axis_size("wave")
    tile_pos = lax.axis_index("tile")
    wave_pos = lax.axis_index("wave")
    south = {"tile": lax.rem(tile_pos + 1, tile_count)}
    north = {"tile": lax.rem(tile_pos + tile_count - 1, tile_count)}
    above = {"wave": lax.rem(wave_pos + 1, wave_count)}
    below = {"wave": lax.rem(wave_pos + wave_count - 1, wave_count)}

    barrier = pltpu.get_barrier_semaphore()
    for other in (south, north, above, below):
        pl.semaphore_signal(barrier, inc=1, device_id=other, device_id_type=MESH)

    def remote(source, target, send, recv, device):
        return pltpu.make_async_remote_copy(
            src_ref=source, dst_ref=target, send_sem=send, recv_sem=recv,
            device_id=device, device_id_type=MESH,
        )

    sources = [(fields_in.at[k], fields.at[k]) for k in range(per_group)] + [
        (sigma_in, sigma), (wavenumbers_in, wavenumbers), (weights_in, weights),
        (counts_in, counts), (electrodes_in, electrodes), (pairs_in, pairs)]
    loads = [
        pltpu.make_async_copy(source, target, in_sem.at[place]) for place, (source, target) in enumerate(sources)]
    for load in loads:
        load.start()
    sig_south = remote(sigma_in.at[pl.ds(ROWS - HALO, HALO)], sig_n, s_send.at[0], s_recv.at[0], south)
    sig_north = remote(sigma_in.at[pl.ds(0, HALO)], sig_s, s_send.at[1], s_recv.at[1], north)
    pl.semaphore_wait(barrier, 4)
    sig_south.start()
    sig_north.start()

    lane = lax.broadcasted_iota(jnp.int32, (SUBS, LANES), 1)
    sub = lax.broadcasted_iota(jnp.int32, (SUBS, LANES), 0)
    first_lane = lane == 0
    last_lane = lane == LANES - 1
    zero = jnp.zeros((SUBS, LANES), F32)

    @pl.loop(0, PARTS)
    def _(block):
        wide = PARTS * LANES
        base = pl.multiple_of(block * LANES, LANES)
        row = lax.broadcasted_iota(jnp.int32, (LANES, wide), 0) + base
        column = lax.broadcasted_iota(jnp.int32, (LANES, wide), 1)
        into[pl.ds(base, LANES), :] = jnp.where(
            row == lax.rem(column, LANES) * PARTS + lax.div(column, LANES), 1.0, 0.0).astype(BF16)
        back[pl.ds(base, LANES), :] = jnp.where(
            column == lax.rem(row, LANES) * PARTS + lax.div(row, LANES), 1.0, 0.0).astype(BF16)

    row = lax.broadcasted_iota(jnp.int32, weave.shape, 0)
    column = lax.broadcasted_iota(jnp.int32, weave.shape, 1)
    weave[...] = jnp.where(
        column == lax.rem(row, SUBS) * ROWS + lax.div(row, SUBS), 1.0, 0.0).astype(BF16)

    for part in range(PARTS):
        rows8 = pl.ds(part * SUBS, SUBS)
        for row in range(LAST, SPAN):
            an[row, rows8, :] = zero
            aw[row, rows8, :] = zero
            src[0, row] = zero
            for buf in range(2):
                w[buf, row, rows8, :] = zero
        for edge in (0, LAST):
            sig[part, pl.ds(edge, FIRST), :] = zero + 1.0

    for load in loads:
        load.wait()
    def halo_copies(pair):
        return (
            remote(stage.at[pair, pl.ds(ROWS * SUBS, HALO * SUBS)], stage.at[pair, pl.ds(0, HALO * SUBS)],
                   h_send.at[0, pair], h_recv.at[0, pair], south),
            remote(stage.at[pair, pl.ds(HALO * SUBS, HALO * SUBS)],
                   stage.at[pair, pl.ds((HALO + ROWS) * SUBS, HALO * SUBS)],
                   h_send.at[1, pair], h_recv.at[1, pair], north),
        )

    @pl.loop(0, 2)
    def _(batch):
        woven = []
        for pair in (2 * batch, 2 * batch + 1):
            columns = [slot_column(pair, half, wave_pos) for half in range(2)]
            block = jnp.concatenate(
                [fields[k, columns[half]] for half in range(2) for k in range(per_group)], axis=0)
            woven.append(jnp.dot(weave[...], block, preferred_element_type=F32).astype(BF16))
        moved = jnp.dot(jnp.concatenate(woven, axis=0), into[...], preferred_element_type=F32).astype(BF16)
        for place, pair in enumerate((2 * batch, 2 * batch + 1)):
            stage[pair, pl.ds(HALO * SUBS, ROWS * SUBS), :] = moved[place * ROWS * SUBS:(place + 1) * ROWS * SUBS]
            for copy in halo_copies(pair):
                copy.start()

    def by_wavenumber(scalars):
        value = zero
        for k, scalar in enumerate(scalars):
            value = jnp.where(lax.rem(sub, per_group) == k, scalar, value)
        return value

    def everywhere(scalars):
        return jnp.concatenate([by_wavenumber(scalars)] * PARTS, axis=0)

    group = [wave_pos * per_group + k for k in range(per_group)]
    square = by_wavenumber([wavenumbers[g] * wavenumbers[g] for g in group])
    final = by_wavenumber([
        weights[g] * chosen(counts[g], [1.0 / tau for tau in TAU[: ITERS + 1]]) for g in group])
    for step in range(ITERS):
        live = [step - (ITERS - counts[g]) for g in group]
        vectors[3 * step] = everywhere([
            jnp.where(at < 0, F32(2.0), jnp.where(at == 0, F32(1.0 + 0.5 * OMEGA), F32(OMEGA))) for at in live])
        vectors[3 * step + 1] = everywhere([
            jnp.where(at < 0, F32(0.0), jnp.where(at == 0, F32(0.5), F32(1.0))) for at in live])
        vectors[3 * step + 2] = everywhere([chosen(at, [0.5] + TAU[1:ITERS]) for at in live])

    sig_south.wait_recv()
    sig_north.wait_recv()
    whole = jnp.concatenate([sig_n[...], sigma[...], sig_s[...]], axis=0)
    moved = jnp.dot(jnp.concatenate(thirds(whole), axis=0), into[...], preferred_element_type=F32)
    moved = (moved[:HELD] + moved[HELD:2 * HELD]) + moved[2 * HELD:]
    for part in range(PARTS):
        sig[part, pl.ds(FIRST, HELD), :] = moved[:, part * LANES:(part + 1) * LANES]

    @pl.loop(1, LAST // SUBS)
    def _(row_tile):
        row = pl.multiple_of(row_tile * SUBS, SUBS)
        place = tile_pos * ROWS + row - CORE + sub
        last_row = tile_count * ROWS
        centre = [sig[part, pl.ds(row, SUBS), :] for part in range(PARTS)]
        for part in range(PARTS):
            mid = centre[part]
            up = jnp.where(place == 0, 0.0, sig[part, pl.ds(row - 1, SUBS), :])
            down = jnp.where(place == last_row - 1, 0.0, sig[part, pl.ds(row + 1, SUBS), :])
            if part == 0:
                left = jnp.where(first_lane, 0.0, pltpu.roll(centre[-1], 1, 1))
            else:
                left = centre[part - 1]
            if part == PARTS - 1:
                right = jnp.where(last_lane, 0.0, pltpu.roll(centre[0], LANES - 1, 1))
            else:
                right = centre[part + 1]
            faces = [0.5 * (mid + near) for near in (up, down, left, right)]
            diag[part, pl.ds(row, SUBS), :] = (faces[0] + faces[1]) + (faces[2] + faces[3])
            outside = jnp.logical_or(place == 0, place == last_row)
            face_n[part, pl.ds(row, SUBS), :] = jnp.where(outside, 0.0, (2.0 / DELTA) * faces[0])
            west = (2.0 / DELTA) * faces[2]
            if part == 0:
                west = jnp.where(first_lane, 0.0, west)
            face_w[part, pl.ds(row, SUBS), :] = west

    def couplings(row, above_row):
        def spread(ref, part):
            return jnp.broadcast_to(ref[part, pl.ds(row, 1), :], (SUBS, LANES))

        here = []
        for part in range(PARTS):
            rows8 = pl.ds(part * SUBS, SUBS)
            value = spread(diag, part) + square * spread(sig, part)
            guess = lax.rsqrt(value)
            root[row, rows8, :] = value * guess
            close[row, rows8, :] = final * guess
            an[row, rows8, :] = spread(face_n, part) * (guess * above_row[part])
            here.append(guess)
        src[1, row] = here[0]
        for part in range(PARTS):
            beside = here[part - 1] if part else pltpu.roll(here[-1], 1, 1)
            aw[row, pl.ds(part * SUBS, SUBS), :] = spread(face_w, part) * (here[part] * beside)
        return tuple(here)

    def four_rows(block, above_row):
        for place in range(4):
            above_row = couplings(FIRST + 4 * block + place, above_row)
        return above_row

    lax.fori_loop(0, HELD // 4, four_rows, (zero,) * PARTS)

    def sweep(step):
        now, later = step % 2, (step + 1) % 2
        before = now if step == 0 else later
        charge = vectors[3 * step + 2, pl.ds(0, SUBS), :]
        start = FIRST + step + 1
        unroll, blocks = UNROLL[step]
        parts = [pl.ds(part * SUBS, SUBS) for part in range(PARTS)]

        def one(row, carry):
            old, sums = carry
            edge = pltpu.roll(w[now, row, parts[-1], :], 1, 1)
            u, held, flow_first = [], [], None
            for part, at in enumerate(parts):
                here = w[now, row, at, :]
                north_c = an[row, at, :]
                side_gain, centre_gain = vectors[3 * step + 1, at, :], vectors[3 * step, at, :]
                value = side_gain * (sums[part] + north_c * here) + (
                    centre_gain * old[part] - w[before, row - 1, at, :])
                if part == 0:
                    value = value + charge * src[0, row - 1]
                w[later, row - 1, at, :] = value
                west_c = aw[row, at, :]
                flow = west_c * here
                if part == 0:
                    flow_first = pltpu.roll(flow, LANES - 1, 1)
                else:
                    held[-1] = held[-1] + flow
                held.append(north_c * old[part] + west_c * (u[-1] if part else edge))
                u.append(here)
            held[-1] = held[-1] + flow_first
            return tuple(u), tuple(held)

        def body(block, carry):
            for place in range(unroll):
                carry = one(start + unroll * block + place, carry)
            return carry

        opening = tuple(w[now, start - 1, at, :] for at in parts)
        lax.fori_loop(0, blocks, body, (opening, (zero,) * PARTS))

    def rs_copies(pair):
        slot = 2 * pair
        return (
            remote(acc.at[slot], from_low.at[pair], r_send.at[0, pair], r_recv.at[0, pair], above),
            remote(acc.at[slot + 1], from_high.at[pair], r_send.at[1, pair], r_recv.at[1, pair], below),
        )

    @pl.loop(0, 4)
    def _(pair):
        columns = [slot_column(pair, half, wave_pos) for half in range(2)]
        spots = []
        for end in range(2):
            low, high = [electrodes[pairs[end, column]] for column in columns]
            spots.append(jnp.where(sub < per_group, low, high) - tile_pos * ROWS + CORE)
        for copy in halo_copies(pair):
            copy.wait_recv()

        @pl.loop(0, HELD // 4)
        def _(block):
            for twin in (2 * block, 2 * block + 1):
                for part in range(PARTS):
                    rows8 = pl.ds(part * SUBS, SUBS)
                    given = stage[pair, pl.ds(twin * 2 * SUBS, 2 * SUBS), pl.ds(part * LANES, LANES)].astype(F32)
                    for place in range(2):
                        row = FIRST + 2 * twin + place
                        w[0, row, rows8, :] = given[place * SUBS:(place + 1) * SUBS] * root[row, rows8, :]
            for place in range(4):
                row = FIRST + 4 * block + place
                spot = jnp.where(row == spots[0], CURRENT, 0.0) - jnp.where(row == spots[1], CURRENT, 0.0)
                spot = (2.0 / DELTA) * spot * src[1, row]
                src[0, row] = jnp.where(first_lane, spot, 0.0)

        for step in range(ITERS):
            sweep(step)

        @pl.loop(0, ROWS // 4)
        def _(block):
            for row in [4 * block + place for place in range(4)]:
                for part in range(PARTS):
                    rows8 = pl.ds(part * SUBS, SUBS)
                    value = close[CORE + row, rows8, :] * w[ITERS % 2, CORE + row, rows8, :]
                    value = value + pltpu.roll(value, SUBS - 2, 0)
                    value = value + pltpu.roll(value, SUBS - 1, 0)
                    for half in range(2):
                        acc[2 * pair + half, part, pl.ds(row, 1), :] = value[half * per_group:half * per_group + 1]

        @pl.when(pair == 1)
        def _():
            rs_copies(0)[0].wait_recv()
            acc[2] += from_low[0]

        @pl.when(pair == 2)
        def _():
            rs_copies(0)[1].wait_recv()
            acc[5] += from_high[0]

        @pl.when(pair < 3)
        def _():
            for copy in rs_copies(pair):
                copy.start()

    for pair in (1, 2):
        for copy in rs_copies(pair):
            copy.wait_recv()
    total = jnp.concatenate([
        jnp.concatenate([acc[6 + half, part] + (from_low[1 + half, part] + from_high[1 + half, part])
                         for part in range(PARTS)], axis=1)
        for half in range(2)], axis=0)
    moved = jnp.dot(jnp.concatenate(thirds(total), axis=0), back[...], preferred_element_type=F32)
    for half in range(2):
        cut = half * ROWS
        out[half] = (moved[cut:cut + ROWS] + moved[2 * ROWS + cut:3 * ROWS + cut]) + moved[
            4 * ROWS + cut:5 * ROWS + cut]

    for pair in range(3):
        for copy in rs_copies(pair):
            copy.wait_send()
    for pair in range(4):
        for copy in halo_copies(pair):
            copy.wait_send()
    sig_south.wait_send()
    sig_north.wait_send()


def local(*arrays):
    arrays = (*arrays[:-1], arrays[-1].T)
    fields = arrays[0]
    per_group, sources, rows, depth = fields.shape
    small = [pltpu.SMEM(a.shape, a.dtype) for a in arrays[2:]]
    tall = pltpu.VMEM((SPAN, PARTS * SUBS, LANES), F32)
    flat = pltpu.VMEM((PARTS, SPAN, LANES), F32)
    return pl.pallas_call(
        kernel,
        out_shape=jax.ShapeDtypeStruct((sources // 4, rows, depth), F32),
        in_specs=[pl.BlockSpec(memory_space=pltpu.HBM)] * len(arrays),
        out_specs=pl.BlockSpec(memory_space=pltpu.VMEM),
        scratch_shapes=[
            pltpu.VMEM(fields.shape, fields.dtype),
            pltpu.VMEM((rows, depth), F32),
            *small,
            pltpu.VMEM((depth, depth), BF16),
            pltpu.VMEM((depth, depth), BF16),
            pltpu.VMEM((SUBS * rows, SUBS * rows), BF16),
            pltpu.VMEM((4, HELD * SUBS, depth), BF16),
            pltpu.VMEM((HALO, depth), F32),
            pltpu.VMEM((HALO, depth), F32),
            flat, flat, flat, flat,
            tall, tall, tall, tall,
            pltpu.VMEM((3 * ITERS, PARTS * SUBS, LANES), F32),
            pltpu.VMEM((2, SPAN, SUBS, LANES), F32),
            pltpu.VMEM((2, SPAN, PARTS * SUBS, LANES), F32),
            pltpu.VMEM((sources, PARTS, rows, LANES), F32),
            pltpu.VMEM((3, PARTS, rows, LANES), F32),
            pltpu.VMEM((3, PARTS, rows, LANES), F32),
            pltpu.SemaphoreType.DMA((10,)),
            pltpu.SemaphoreType.DMA((2, 4)),
            pltpu.SemaphoreType.DMA((2, 4)),
            pltpu.SemaphoreType.DMA((2,)),
            pltpu.SemaphoreType.DMA((2,)),
            pltpu.SemaphoreType.DMA((2, 3)),
            pltpu.SemaphoreType.DMA((2, 3)),
        ],
        compiler_params=pltpu.CompilerParams(
            collective_id=0, has_side_effects=True, vmem_limit_bytes=63 * 1024 * 1024),
    )(*arrays)


def solution(mesh):
    placed = (P("wave", None, "tile", None), P("tile", None), P(), P(), P(), P(), P())
    return jax.shard_map(
        local, mesh=mesh, in_specs=placed, out_specs=P("wave", "tile", None), check_vma=False
    )
```

```python
import jax
import jax.numpy as jnp
from jax import lax
from jax.experimental import pallas as pl
from jax.experimental.pallas import tpu as pltpu
from jax.sharding import PartitionSpec as P

ITERS = 8
LOWER = 0.1
UPPER = 2.0
THETA = (UPPER + LOWER) / 2.0
DELTA = (UPPER - LOWER) / 2.0
SIGMA_ONE = THETA / DELTA
CURRENT = 2.0

TAU = [1.0, SIGMA_ONE]
for _ in range(ITERS):
    TAU.append(2.0 * SIGMA_ONE * TAU[-1] - TAU[-2])
OMEGA = 2.0 * (THETA - 1.0) / DELTA

LANES = 128
SUBS = 8
PARTS = 8
ROWS = 32
HALO = 8
HELD = ROWS + 2 * HALO
SPAN = 64
FIRST = 8
CORE = FIRST + HALO
LAST = FIRST + HELD
UNROLL = ((8, 6), (9, 5), (11, 4), (7, 6), (8, 5), (8, 5), (7, 5), (11, 3))
MESH = pl.DeviceIdType.MESH
F32 = jnp.float32
BF16 = jnp.bfloat16


def chosen(index, table):
    value = jnp.float32(0.0)
    for position, entry in enumerate(table):
        value = jnp.where(index == position, jnp.float32(entry), value)
    return value


def slot_column(pair, half, wave_pos):
    middle = jnp.logical_or(pair == 1, pair == 2)
    ahead = jnp.where(pair == 0, 2, jnp.where(middle, 1 + 2 * half, 0))
    offset = jnp.where(middle, pair - 1, half)
    return 2 * lax.rem(wave_pos + ahead, 4) + offset


def thirds(values):
    high = values.astype(BF16)
    rest = values - high.astype(F32)
    middle = rest.astype(BF16)
    low = (rest - middle.astype(F32)).astype(BF16)
    return high, middle, low


def kernel(
    fields_in, sigma_in, wavenumbers_in, weights_in, counts_in, electrodes_in, pairs_in, out,
    fields, sigma, wavenumbers, weights, counts, electrodes, pairs,
    into, back, weave, stage, sig_n, sig_s, sig, diag, face_n, face_w,
    an, aw, root, close, vectors, src, w, acc, from_low, from_high,
    in_sem, h_send, h_recv, s_send, s_recv, r_send, r_recv,
):
    per_group = fields.shape[0]
    tile_count = lax.axis_size("tile")
    wave_count = lax.axis_size("wave")
    tile_pos = lax.axis_index("tile")
    wave_pos = lax.axis_index("wave")
    south = {"tile": lax.rem(tile_pos + 1, tile_count)}
    north = {"tile": lax.rem(tile_pos + tile_count - 1, tile_count)}
    above = {"wave": lax.rem(wave_pos + 1, wave_count)}
    below = {"wave": lax.rem(wave_pos + wave_count - 1, wave_count)}

    barrier = pltpu.get_barrier_semaphore()
    for other in (south, north, above, below):
        pl.semaphore_signal(barrier, inc=1, device_id=other, device_id_type=MESH)

    def remote(source, target, send, recv, device):
        return pltpu.make_async_remote_copy(
            src_ref=source, dst_ref=target, send_sem=send, recv_sem=recv,
            device_id=device, device_id_type=MESH,
        )

    sources = [(fields_in.at[k], fields.at[k]) for k in range(per_group)] + [
        (sigma_in, sigma), (wavenumbers_in, wavenumbers), (weights_in, weights),
        (counts_in, counts), (electrodes_in, electrodes), (pairs_in, pairs)]
    loads = [
        pltpu.make_async_copy(source, target, in_sem.at[place]) for place, (source, target) in enumerate(sources)]
    for load in loads:
        load.start()
    sig_south = remote(sigma_in.at[pl.ds(ROWS - HALO, HALO)], sig_n, s_send.at[0], s_recv.at[0], south)
    sig_north = remote(sigma_in.at[pl.ds(0, HALO)], sig_s, s_send.at[1], s_recv.at[1], north)

    lane = lax.broadcasted_iota(jnp.int32, (SUBS, LANES), 1)
    sub = lax.broadcasted_iota(jnp.int32, (SUBS, LANES), 0)
    first_lane = lane == 0
    last_lane = lane == LANES - 1
    zero = jnp.zeros((SUBS, LANES), F32)

    @pl.loop(0, PARTS)
    def _(block):
        wide = PARTS * LANES
        base = pl.multiple_of(block * LANES, LANES)
        row = lax.broadcasted_iota(jnp.int32, (LANES, wide), 0) + base
        column = lax.broadcasted_iota(jnp.int32, (LANES, wide), 1)
        into[pl.ds(base, LANES), :] = jnp.where(
            row == lax.rem(column, LANES) * PARTS + lax.div(column, LANES), 1.0, 0.0).astype(BF16)
        back[pl.ds(base, LANES), :] = jnp.where(
            column == lax.rem(row, LANES) * PARTS + lax.div(row, LANES), 1.0, 0.0).astype(BF16)

    row = lax.broadcasted_iota(jnp.int32, weave.shape, 0)
    column = lax.broadcasted_iota(jnp.int32, weave.shape, 1)
    weave[...] = jnp.where(
        column == lax.rem(row, SUBS) * ROWS + lax.div(row, SUBS), 1.0, 0.0).astype(BF16)

    for part in range(PARTS):
        rows8 = pl.ds(part * SUBS, SUBS)
        for row in range(LAST, SPAN):
            an[row, rows8, :] = zero
            aw[row, rows8, :] = zero
            src[0, row] = zero
            for buf in range(2):
                w[buf, row, rows8, :] = zero
        for edge in (0, LAST):
            sig[part, pl.ds(edge, FIRST), :] = zero + 1.0

    pl.semaphore_wait(barrier, 4)
    sig_south.start()
    sig_north.start()

    for load in loads:
        load.wait()
    def halo_copies(pair):
        return (
            remote(stage.at[pair, pl.ds(ROWS * SUBS, HALO * SUBS)], stage.at[pair, pl.ds(0, HALO * SUBS)],
                   h_send.at[0, pair], h_recv.at[0, pair], south),
            remote(stage.at[pair, pl.ds(HALO * SUBS, HALO * SUBS)],
                   stage.at[pair, pl.ds((HALO + ROWS) * SUBS, HALO * SUBS)],
                   h_send.at[1, pair], h_recv.at[1, pair], north),
        )

    @pl.loop(0, 2)
    def _(batch):
        woven = []
        for pair in (2 * batch, 2 * batch + 1):
            columns = [slot_column(pair, half, wave_pos) for half in range(2)]
            block = jnp.concatenate(
                [fields[k, columns[half]] for half in range(2) for k in range(per_group)], axis=0)
            woven.append(jnp.dot(weave[...], block, preferred_element_type=F32).astype(BF16))
        moved = jnp.dot(jnp.concatenate(woven, axis=0), into[...], preferred_element_type=F32).astype(BF16)
        for place, pair in enumerate((2 * batch, 2 * batch + 1)):
            stage[pair, pl.ds(HALO * SUBS, ROWS * SUBS), :] = moved[place * ROWS * SUBS:(place + 1) * ROWS * SUBS]
            for copy in halo_copies(pair):
                copy.start()

    def by_wavenumber(scalars):
        value = zero
        for k, scalar in enumerate(scalars):
            value = jnp.where(lax.rem(sub, per_group) == k, scalar, value)
        return value

    def everywhere(scalars):
        return jnp.concatenate([by_wavenumber(scalars)] * PARTS, axis=0)

    group = [wave_pos * per_group + k for k in range(per_group)]
    square = by_wavenumber([wavenumbers[g] * wavenumbers[g] for g in group])
    final = by_wavenumber([
        weights[g] * chosen(counts[g], [1.0 / tau for tau in TAU[: ITERS + 1]]) for g in group])
    for step in range(ITERS):
        live = [step - (ITERS - counts[g]) for g in group]
        vectors[3 * step] = everywhere([
            jnp.where(at < 0, F32(2.0), jnp.where(at == 0, F32(1.0 + 0.5 * OMEGA), F32(OMEGA))) for at in live])
        vectors[3 * step + 1] = everywhere([
            jnp.where(at < 0, F32(0.0), jnp.where(at == 0, F32(0.5), F32(1.0))) for at in live])
        vectors[3 * step + 2] = everywhere([chosen(at, [0.5] + TAU[1:ITERS]) for at in live])

    sig_south.wait_recv()
    sig_north.wait_recv()
    whole = jnp.concatenate([sig_n[...], sigma[...], sig_s[...]], axis=0)
    moved = jnp.dot(jnp.concatenate(thirds(whole), axis=0), into[...], preferred_element_type=F32)
    moved = (moved[:HELD] + moved[HELD:2 * HELD]) + moved[2 * HELD:]
    for part in range(PARTS):
        sig[part, pl.ds(FIRST, HELD), :] = moved[:, part * LANES:(part + 1) * LANES]

    @pl.loop(1, LAST // SUBS)
    def _(row_tile):
        row = pl.multiple_of(row_tile * SUBS, SUBS)
        place = tile_pos * ROWS + row - CORE + sub
        last_row = tile_count * ROWS
        centre = [sig[part, pl.ds(row, SUBS), :] for part in range(PARTS)]
        for part in range(PARTS):
            mid = centre[part]
            up = jnp.where(place == 0, 0.0, sig[part, pl.ds(row - 1, SUBS), :])
            down = jnp.where(place == last_row - 1, 0.0, sig[part, pl.ds(row + 1, SUBS), :])
            if part == 0:
                left = jnp.where(first_lane, 0.0, pltpu.roll(centre[-1], 1, 1))
            else:
                left = centre[part - 1]
            if part == PARTS - 1:
                right = jnp.where(last_lane, 0.0, pltpu.roll(centre[0], LANES - 1, 1))
            else:
                right = centre[part + 1]
            faces = [0.5 * (mid + near) for near in (up, down, left, right)]
            diag[part, pl.ds(row, SUBS), :] = (faces[0] + faces[1]) + (faces[2] + faces[3])
            outside = jnp.logical_or(place == 0, place == last_row)
            face_n[part, pl.ds(row, SUBS), :] = jnp.where(outside, 0.0, (2.0 / DELTA) * faces[0])
            west = (2.0 / DELTA) * faces[2]
            if part == 0:
                west = jnp.where(first_lane, 0.0, west)
            face_w[part, pl.ds(row, SUBS), :] = west

    def couplings(row, above_row):
        def spread(ref, part):
            return jnp.broadcast_to(ref[part, pl.ds(row, 1), :], (SUBS, LANES))

        here = []
        for part in range(PARTS):
            rows8 = pl.ds(part * SUBS, SUBS)
            value = spread(diag, part) + square * spread(sig, part)
            guess = lax.rsqrt(value)
            root[row, rows8, :] = value * guess
            close[row, rows8, :] = final * guess
            an[row, rows8, :] = spread(face_n, part) * (guess * above_row[part])
            here.append(guess)
        src[1, row] = here[0]
        for part in range(PARTS):
            beside = here[part - 1] if part else pltpu.roll(here[-1], 1, 1)
            aw[row, pl.ds(part * SUBS, SUBS), :] = spread(face_w, part) * (here[part] * beside)
        return tuple(here)

    def four_rows(block, above_row):
        for place in range(4):
            above_row = couplings(FIRST + 4 * block + place, above_row)
        return above_row

    lax.fori_loop(0, HELD // 4, four_rows, (zero,) * PARTS)

    def sweep(step):
        now, later = step % 2, (step + 1) % 2
        before = now if step == 0 else later
        charge = vectors[3 * step + 2, pl.ds(0, SUBS), :]
        start = FIRST + step + 1
        unroll, blocks = UNROLL[step]
        parts = [pl.ds(part * SUBS, SUBS) for part in range(PARTS)]

        def one(row, carry):
            old, sums = carry
            edge = pltpu.roll(w[now, row, parts[-1], :], 1, 1)
            u, held, flow_first = [], [], None
            for part, at in enumerate(parts):
                here = w[now, row, at, :]
                north_c = an[row, at, :]
                side_gain, centre_gain = vectors[3 * step + 1, at, :], vectors[3 * step, at, :]
                value = side_gain * (sums[part] + north_c * here) + (
                    centre_gain * old[part] - w[before, row - 1, at, :])
                if part == 0:
                    value = value + charge * src[0, row - 1]
                w[later, row - 1, at, :] = value
                west_c = aw[row, at, :]
                flow = west_c * here
                if part == 0:
                    flow_first = pltpu.roll(flow, LANES - 1, 1)
                else:
                    held[-1] = held[-1] + flow
                held.append(north_c * old[part] + west_c * (u[-1] if part else edge))
                u.append(here)
            held[-1] = held[-1] + flow_first
            return tuple(u), tuple(held)

        def body(block, carry):
            for place in range(unroll):
                carry = one(start + unroll * block + place, carry)
            return carry

        opening = tuple(w[now, start - 1, at, :] for at in parts)
        lax.fori_loop(0, blocks, body, (opening, (zero,) * PARTS))

    def rs_copies(pair):
        slot = 2 * pair
        return (
            remote(acc.at[slot], from_low.at[pair], r_send.at[0, pair], r_recv.at[0, pair], above),
            remote(acc.at[slot + 1], from_high.at[pair], r_send.at[1, pair], r_recv.at[1, pair], below),
        )

    @pl.loop(0, 4)
    def _(pair):
        columns = [slot_column(pair, half, wave_pos) for half in range(2)]
        spots = []
        for end in range(2):
            low, high = [electrodes[pairs[end, column]] for column in columns]
            spots.append(jnp.where(sub < per_group, low, high) - tile_pos * ROWS + CORE)
        for copy in halo_copies(pair):
            copy.wait_recv()

        @pl.loop(0, HELD // 4)
        def _(block):
            for twin in (2 * block, 2 * block + 1):
                for part in range(PARTS):
                    rows8 = pl.ds(part * SUBS, SUBS)
                    given = stage[pair, pl.ds(twin * 2 * SUBS, 2 * SUBS), pl.ds(part * LANES, LANES)].astype(F32)
                    for place in range(2):
                        row = FIRST + 2 * twin + place
                        w[0, row, rows8, :] = given[place * SUBS:(place + 1) * SUBS] * root[row, rows8, :]
            for place in range(4):
                row = FIRST + 4 * block + place
                spot = jnp.where(row == spots[0], CURRENT, 0.0) - jnp.where(row == spots[1], CURRENT, 0.0)
                spot = (2.0 / DELTA) * spot * src[1, row]
                src[0, row] = jnp.where(first_lane, spot, 0.0)

        for step in range(ITERS):
            sweep(step)

        @pl.loop(0, ROWS // 4)
        def _(block):
            for row in [4 * block + place for place in range(4)]:
                for part in range(PARTS):
                    rows8 = pl.ds(part * SUBS, SUBS)
                    value = close[CORE + row, rows8, :] * w[ITERS % 2, CORE + row, rows8, :]
                    value = value + pltpu.roll(value, SUBS - 2, 0)
                    value = value + pltpu.roll(value, SUBS - 1, 0)
                    for half in range(2):
                        acc[2 * pair + half, part, pl.ds(row, 1), :] = value[half * per_group:half * per_group + 1]

        @pl.when(pair == 1)
        def _():
            rs_copies(0)[0].wait_recv()
            acc[2] += from_low[0]

        @pl.when(pair == 2)
        def _():
            rs_copies(0)[1].wait_recv()
            acc[5] += from_high[0]

        @pl.when(pair < 3)
        def _():
            for copy in rs_copies(pair):
                copy.start()

    for pair in (1, 2):
        for copy in rs_copies(pair):
            copy.wait_recv()
    total = jnp.concatenate([
        jnp.concatenate([acc[6 + half, part] + (from_low[1 + half, part] + from_high[1 + half, part])
                         for part in range(PARTS)], axis=1)
        for half in range(2)], axis=0)
    moved = jnp.dot(jnp.concatenate(thirds(total), axis=0), back[...], preferred_element_type=F32)
    for half in range(2):
        cut = half * ROWS
        out[half] = (moved[cut:cut + ROWS] + moved[2 * ROWS + cut:3 * ROWS + cut]) + moved[
            4 * ROWS + cut:5 * ROWS + cut]

    for pair in range(3):
        for copy in rs_copies(pair):
            copy.wait_send()
    for pair in range(4):
        for copy in halo_copies(pair):
            copy.wait_send()
    sig_south.wait_send()
    sig_north.wait_send()


def local(*arrays):
    arrays = (*arrays[:-1], arrays[-1].T)
    fields = arrays[0]
    per_group, sources, rows, depth = fields.shape
    small = [pltpu.SMEM(a.shape, a.dtype) for a in arrays[2:]]
    tall = pltpu.VMEM((SPAN, PARTS * SUBS, LANES), F32)
    flat = pltpu.VMEM((PARTS, SPAN, LANES), F32)
    return pl.pallas_call(
        kernel,
        out_shape=jax.ShapeDtypeStruct((sources // 4, rows, depth), F32),
        in_specs=[pl.BlockSpec(memory_space=pltpu.HBM)] * len(arrays),
        out_specs=pl.BlockSpec(memory_space=pltpu.VMEM),
        scratch_shapes=[
            pltpu.VMEM(fields.shape, fields.dtype),
            pltpu.VMEM((rows, depth), F32),
            *small,
            pltpu.VMEM((depth, depth), BF16),
            pltpu.VMEM((depth, depth), BF16),
            pltpu.VMEM((SUBS * rows, SUBS * rows), BF16),
            pltpu.VMEM((4, HELD * SUBS, depth), BF16),
            pltpu.VMEM((HALO, depth), F32),
            pltpu.VMEM((HALO, depth), F32),
            flat, flat, flat, flat,
            tall, tall, tall, tall,
            pltpu.VMEM((3 * ITERS, PARTS * SUBS, LANES), F32),
            pltpu.VMEM((2, SPAN, SUBS, LANES), F32),
            pltpu.VMEM((2, SPAN, PARTS * SUBS, LANES), F32),
            pltpu.VMEM((sources, PARTS, rows, LANES), F32),
            pltpu.VMEM((3, PARTS, rows, LANES), F32),
            pltpu.VMEM((3, PARTS, rows, LANES), F32),
            pltpu.SemaphoreType.DMA((10,)),
            pltpu.SemaphoreType.DMA((2, 4)),
            pltpu.SemaphoreType.DMA((2, 4)),
            pltpu.SemaphoreType.DMA((2,)),
            pltpu.SemaphoreType.DMA((2,)),
            pltpu.SemaphoreType.DMA((2, 3)),
            pltpu.SemaphoreType.DMA((2, 3)),
        ],
        compiler_params=pltpu.CompilerParams(
            collective_id=0, has_side_effects=True, vmem_limit_bytes=63 * 1024 * 1024),
    )(*arrays)


def solution(mesh):
    placed = (P("wave", None, "tile", None), P("tile", None), P(), P(), P(), P(), P())
    return jax.shard_map(
        local, mesh=mesh, in_specs=placed, out_specs=P("wave", "tile", None), check_vma=False
    )
```

```python
import jax
import jax.numpy as jnp
from jax import lax
from jax.experimental import pallas as pl
from jax.experimental.pallas import tpu as pltpu
from jax.sharding import PartitionSpec as P

ITERS = 8
LOWER = 0.1
UPPER = 2.0
THETA = (UPPER + LOWER) / 2.0
DELTA = (UPPER - LOWER) / 2.0
SIGMA_ONE = THETA / DELTA
CURRENT = 2.0

TAU = [1.0, SIGMA_ONE]
for _ in range(ITERS):
    TAU.append(2.0 * SIGMA_ONE * TAU[-1] - TAU[-2])
OMEGA = 2.0 * (THETA - 1.0) / DELTA

LANES = 128
SUBS = 8
PARTS = 8
ROWS = 32
HALO = 8
HELD = ROWS + 2 * HALO
SPAN = 64
FIRST = 8
CORE = FIRST + HALO
LAST = FIRST + HELD
UNROLL = ((8, 6), (9, 5), (11, 4), (7, 6), (13, 3), (19, 2), (7, 5), (11, 3))
FIRST_TWINS = 11
MESH = pl.DeviceIdType.MESH
F32 = jnp.float32
BF16 = jnp.bfloat16


def chosen(index, table):
    value = jnp.float32(0.0)
    for position, entry in enumerate(table):
        value = jnp.where(index == position, jnp.float32(entry), value)
    return value


def slot_column(pair, half, wave_pos):
    middle = jnp.logical_or(pair == 1, pair == 2)
    ahead = jnp.where(pair == 0, 2, jnp.where(middle, 1 + 2 * half, 0))
    offset = jnp.where(middle, pair - 1, half)
    return 2 * lax.rem(wave_pos + ahead, 4) + offset


def thirds(values):
    high = values.astype(BF16)
    rest = values - high.astype(F32)
    middle = rest.astype(BF16)
    low = (rest - middle.astype(F32)).astype(BF16)
    return high, middle, low


def kernel(
    fields_in, sigma_in, wavenumbers_in, weights_in, counts_in, electrodes_in, pairs_in, out,
    fields, sigma, wavenumbers, weights, counts, electrodes, pairs,
    into, back, weave, stage, sig_n, sig_s, sig, diag, face_n, face_w,
    an, aw, root, close, vectors, src, w, acc, from_low, from_high,
    in_sem, h_send, h_recv, s_send, s_recv, r_send, r_recv,
):
    per_group = fields.shape[0]
    tile_count = lax.axis_size("tile")
    wave_count = lax.axis_size("wave")
    tile_pos = lax.axis_index("tile")
    wave_pos = lax.axis_index("wave")
    south = {"tile": lax.rem(tile_pos + 1, tile_count)}
    north = {"tile": lax.rem(tile_pos + tile_count - 1, tile_count)}
    above = {"wave": lax.rem(wave_pos + 1, wave_count)}
    below = {"wave": lax.rem(wave_pos + wave_count - 1, wave_count)}

    barrier = pltpu.get_barrier_semaphore()
    for other in (south, north, above, below):
        pl.semaphore_signal(barrier, inc=1, device_id=other, device_id_type=MESH)

    def remote(source, target, send, recv, device):
        return pltpu.make_async_remote_copy(
            src_ref=source, dst_ref=target, send_sem=send, recv_sem=recv,
            device_id=device, device_id_type=MESH,
        )

    sources = [(fields_in.at[k], fields.at[k]) for k in range(per_group)] + [
        (sigma_in, sigma), (wavenumbers_in, wavenumbers), (weights_in, weights),
        (counts_in, counts), (electrodes_in, electrodes), (pairs_in, pairs)]
    loads = [
        pltpu.make_async_copy(source, target, in_sem.at[place]) for place, (source, target) in enumerate(sources)]
    for load in loads:
        load.start()
    sig_south = remote(sigma_in.at[pl.ds(ROWS - HALO, HALO)], sig_n, s_send.at[0], s_recv.at[0], south)
    sig_north = remote(sigma_in.at[pl.ds(0, HALO)], sig_s, s_send.at[1], s_recv.at[1], north)

    lane = lax.broadcasted_iota(jnp.int32, (SUBS, LANES), 1)
    sub = lax.broadcasted_iota(jnp.int32, (SUBS, LANES), 0)
    first_lane = lane == 0
    last_lane = lane == LANES - 1
    zero = jnp.zeros((SUBS, LANES), F32)

    @pl.loop(0, PARTS)
    def _(block):
        wide = PARTS * LANES
        base = pl.multiple_of(block * LANES, LANES)
        row = lax.broadcasted_iota(jnp.int32, (LANES, wide), 0) + base
        column = lax.broadcasted_iota(jnp.int32, (LANES, wide), 1)
        into[pl.ds(base, LANES), :] = jnp.where(
            row == lax.rem(column, LANES) * PARTS + lax.div(column, LANES), 1.0, 0.0).astype(BF16)
        back[pl.ds(base, LANES), :] = jnp.where(
            column == lax.rem(row, LANES) * PARTS + lax.div(row, LANES), 1.0, 0.0).astype(BF16)

    row = lax.broadcasted_iota(jnp.int32, weave.shape, 0)
    column = lax.broadcasted_iota(jnp.int32, weave.shape, 1)
    weave[...] = jnp.where(
        column == lax.rem(row, SUBS) * ROWS + lax.div(row, SUBS), 1.0, 0.0).astype(BF16)

    for part in range(PARTS):
        rows8 = pl.ds(part * SUBS, SUBS)
        for row in range(LAST, SPAN):
            an[row, rows8, :] = zero
            aw[row, rows8, :] = zero
            src[0, row] = zero
            for buf in range(2):
                w[buf, row, rows8, :] = zero
        for edge in (0, LAST):
            sig[part, pl.ds(edge, FIRST), :] = zero + 1.0

    pl.semaphore_wait(barrier, 4)
    sig_south.start()
    sig_north.start()

    for load in loads:
        load.wait()
    def halo_copies(pair):
        return (
            remote(stage.at[pair, pl.ds(ROWS * SUBS, HALO * SUBS)], stage.at[pair, pl.ds(0, HALO * SUBS)],
                   h_send.at[0, pair], h_recv.at[0, pair], south),
            remote(stage.at[pair, pl.ds(HALO * SUBS, HALO * SUBS)],
                   stage.at[pair, pl.ds((HALO + ROWS) * SUBS, HALO * SUBS)],
                   h_send.at[1, pair], h_recv.at[1, pair], north),
        )

    @pl.loop(0, 2)
    def _(batch):
        woven = []
        for pair in (2 * batch, 2 * batch + 1):
            columns = [slot_column(pair, half, wave_pos) for half in range(2)]
            block = jnp.concatenate(
                [fields[k, columns[half]] for half in range(2) for k in range(per_group)], axis=0)
            woven.append(jnp.dot(weave[...], block, preferred_element_type=F32).astype(BF16))
        moved = jnp.dot(jnp.concatenate(woven, axis=0), into[...], preferred_element_type=F32).astype(BF16)
        for place, pair in enumerate((2 * batch, 2 * batch + 1)):
            stage[pair, pl.ds(HALO * SUBS, ROWS * SUBS), :] = moved[place * ROWS * SUBS:(place + 1) * ROWS * SUBS]
            for copy in halo_copies(pair):
                copy.start()

    def by_wavenumber(scalars):
        value = zero
        for k, scalar in enumerate(scalars):
            value = jnp.where(lax.rem(sub, per_group) == k, scalar, value)
        return value

    def everywhere(scalars):
        return jnp.concatenate([by_wavenumber(scalars)] * PARTS, axis=0)

    group = [wave_pos * per_group + k for k in range(per_group)]
    square = by_wavenumber([wavenumbers[g] * wavenumbers[g] for g in group])
    final = by_wavenumber([
        weights[g] * chosen(counts[g], [1.0 / tau for tau in TAU[: ITERS + 1]]) for g in group])
    for step in range(ITERS):
        live = [step - (ITERS - counts[g]) for g in group]
        vectors[3 * step] = everywhere([
            jnp.where(at < 0, F32(2.0), jnp.where(at == 0, F32(1.0 + 0.5 * OMEGA), F32(OMEGA))) for at in live])
        vectors[3 * step + 1] = everywhere([
            jnp.where(at < 0, F32(0.0), jnp.where(at == 0, F32(0.5), F32(1.0))) for at in live])
        vectors[3 * step + 2] = everywhere([chosen(at, [0.5] + TAU[1:ITERS]) for at in live])

    sig_south.wait_recv()
    sig_north.wait_recv()
    whole = jnp.concatenate([sig_n[...], sigma[...], sig_s[...]], axis=0)
    moved = jnp.dot(jnp.concatenate(thirds(whole), axis=0), into[...], preferred_element_type=F32)
    moved = (moved[:HELD] + moved[HELD:2 * HELD]) + moved[2 * HELD:]
    for part in range(PARTS):
        sig[part, pl.ds(FIRST, HELD), :] = moved[:, part * LANES:(part + 1) * LANES]

    @pl.loop(1, LAST // SUBS)
    def _(row_tile):
        row = pl.multiple_of(row_tile * SUBS, SUBS)
        place = tile_pos * ROWS + row - CORE + sub
        last_row = tile_count * ROWS
        centre = [sig[part, pl.ds(row, SUBS), :] for part in range(PARTS)]
        for part in range(PARTS):
            mid = centre[part]
            up = jnp.where(place == 0, 0.0, sig[part, pl.ds(row - 1, SUBS), :])
            down = jnp.where(place == last_row - 1, 0.0, sig[part, pl.ds(row + 1, SUBS), :])
            if part == 0:
                left = jnp.where(first_lane, 0.0, pltpu.roll(centre[-1], 1, 1))
            else:
                left = centre[part - 1]
            if part == PARTS - 1:
                right = jnp.where(last_lane, 0.0, pltpu.roll(centre[0], LANES - 1, 1))
            else:
                right = centre[part + 1]
            faces = [0.5 * (mid + near) for near in (up, down, left, right)]
            diag[part, pl.ds(row, SUBS), :] = (faces[0] + faces[1]) + (faces[2] + faces[3])
            outside = jnp.logical_or(place == 0, place == last_row)
            face_n[part, pl.ds(row, SUBS), :] = jnp.where(outside, 0.0, (2.0 / DELTA) * faces[0])
            west = (2.0 / DELTA) * faces[2]
            if part == 0:
                west = jnp.where(first_lane, 0.0, west)
            face_w[part, pl.ds(row, SUBS), :] = west

    def couplings(row, above_row):
        def spread(ref, part):
            return jnp.broadcast_to(ref[part, pl.ds(row, 1), :], (SUBS, LANES))

        here = []
        for part in range(PARTS):
            rows8 = pl.ds(part * SUBS, SUBS)
            value = spread(diag, part) + square * spread(sig, part)
            guess = lax.rsqrt(value)
            root[row, rows8, :] = value * guess
            close[row, rows8, :] = final * guess
            an[row, rows8, :] = spread(face_n, part) * (guess * above_row[part])
            here.append(guess)
        src[1, row] = here[0]
        for part in range(PARTS):
            beside = here[part - 1] if part else pltpu.roll(here[-1], 1, 1)
            aw[row, pl.ds(part * SUBS, SUBS), :] = spread(face_w, part) * (here[part] * beside)
        return tuple(here)

    def four_rows(block, above_row):
        for place in range(4):
            above_row = couplings(FIRST + 4 * block + place, above_row)
        return above_row

    lax.fori_loop(0, HELD // 4, four_rows, (zero,) * PARTS)

    def sweep(step, pair, spots):
        now, later = step % 2, (step + 1) % 2
        charge = vectors[3 * step + 2, pl.ds(0, SUBS), :]
        start = FIRST + step + 1
        unroll, blocks = UNROLL[step]
        parts = [pl.ds(part * SUBS, SUBS) for part in range(PARTS)]

        def one(row, carry, u):
            old, sums = carry
            edge = pltpu.roll(u[-1], 1, 1)
            held, flow_first = [], None
            if step == 0:
                spot = jnp.where(row - 1 == spots[0], CURRENT, 0.0) - jnp.where(row - 1 == spots[1], CURRENT, 0.0)
                source = jnp.where(first_lane, (2.0 / DELTA) * spot * src[1, row - 1], 0.0)
                src[0, row - 1] = source
            else:
                source = src[0, row - 1]
            for part, at in enumerate(parts):
                here = u[part]
                north_c = an[row, at, :]
                side_gain, centre_gain = vectors[3 * step + 1, at, :], vectors[3 * step, at, :]
                if step == 0:
                    value = side_gain * (sums[part] + north_c * here) + (centre_gain - 1.0) * old[part]
                else:
                    value = side_gain * (sums[part] + north_c * here) + (
                        centre_gain * old[part] - w[later, row - 1, at, :])
                if part == 0:
                    value = value + charge * source
                w[later, row - 1, at, :] = value
                west_c = aw[row, at, :]
                flow = west_c * here
                if part == 0:
                    flow_first = pltpu.roll(flow, LANES - 1, 1)
                else:
                    held[-1] = held[-1] + flow
                held.append(north_c * old[part] + west_c * (u[part - 1] if part else edge))
            held[-1] = held[-1] + flow_first
            return tuple(u), tuple(held)

        def given(twin):
            both = [[], []]
            for part, at in enumerate(parts):
                values = stage[pair, pl.ds(twin * 2 * SUBS, 2 * SUBS), pl.ds(part * LANES, LANES)].astype(F32)
                for place in range(2):
                    row = FIRST + 2 * twin + place
                    value = values[place * SUBS:(place + 1) * SUBS] * root[row, at, :]
                    w[0, row, at, :] = value
                    both[place].append(value)
            return both

        def two(twin, carry):
            row = FIRST + 2 * twin
            for place, u in enumerate(given(twin)):
                carry = one(row + place, carry, u)
            return carry

        if step == 0:
            opening, second = given(0)
            carry = one(FIRST + 1, (tuple(opening), (zero,) * PARTS), second)
            carry = two(1, carry)

            def several(block, carry):
                for place in range(FIRST_TWINS):
                    carry = two(2 + FIRST_TWINS * block + place, carry)
                return carry

            lax.fori_loop(0, (HELD // 2 - 2) // FIRST_TWINS, several, carry)
        else:

            def body(block, carry):
                for place in range(unroll):
                    row = start + unroll * block + place
                    carry = one(row, carry, [w[now, row, at, :] for at in parts])
                return carry

            opening = tuple(w[now, start - 1, at, :] for at in parts)
            lax.fori_loop(0, blocks, body, (opening, (zero,) * PARTS))

    def rs_copies(pair):
        slot = 2 * pair
        return (
            remote(acc.at[slot], from_low.at[pair], r_send.at[0, pair], r_recv.at[0, pair], above),
            remote(acc.at[slot + 1], from_high.at[pair], r_send.at[1, pair], r_recv.at[1, pair], below),
        )

    @pl.loop(0, 4)
    def _(pair):
        columns = [slot_column(pair, half, wave_pos) for half in range(2)]
        spots = []
        for end in range(2):
            low, high = [electrodes[pairs[end, column]] for column in columns]
            spots.append(jnp.where(sub < per_group, low, high) - tile_pos * ROWS + CORE)
        for copy in halo_copies(pair):
            copy.wait_recv()

        for step in range(ITERS):
            sweep(step, pair, spots)

        @pl.loop(0, ROWS // 4)
        def _(block):
            for row in [4 * block + place for place in range(4)]:
                for part in range(PARTS):
                    rows8 = pl.ds(part * SUBS, SUBS)
                    value = close[CORE + row, rows8, :] * w[ITERS % 2, CORE + row, rows8, :]
                    value = value + pltpu.roll(value, SUBS - 2, 0)
                    value = value + pltpu.roll(value, SUBS - 1, 0)
                    for half in range(2):
                        acc[2 * pair + half, part, pl.ds(row, 1), :] = value[half * per_group:half * per_group + 1]

        @pl.when(pair == 1)
        def _():
            rs_copies(0)[0].wait_recv()
            acc[2] += from_low[0]

        @pl.when(pair == 2)
        def _():
            rs_copies(0)[1].wait_recv()
            acc[5] += from_high[0]

        @pl.when(pair < 3)
        def _():
            for copy in rs_copies(pair):
                copy.start()

    for pair in (1, 2):
        for copy in rs_copies(pair):
            copy.wait_recv()
    total = jnp.concatenate([
        jnp.concatenate([acc[6 + half, part] + (from_low[1 + half, part] + from_high[1 + half, part])
                         for part in range(PARTS)], axis=1)
        for half in range(2)], axis=0)
    moved = jnp.dot(jnp.concatenate(thirds(total), axis=0), back[...], preferred_element_type=F32)
    for half in range(2):
        cut = half * ROWS
        out[half] = (moved[cut:cut + ROWS] + moved[2 * ROWS + cut:3 * ROWS + cut]) + moved[
            4 * ROWS + cut:5 * ROWS + cut]

    for pair in range(3):
        for copy in rs_copies(pair):
            copy.wait_send()
    for pair in range(4):
        for copy in halo_copies(pair):
            copy.wait_send()
    sig_south.wait_send()
    sig_north.wait_send()


def local(*arrays):
    arrays = (*arrays[:-1], arrays[-1].T)
    fields = arrays[0]
    per_group, sources, rows, depth = fields.shape
    small = [pltpu.SMEM(a.shape, a.dtype) for a in arrays[2:]]
    tall = pltpu.VMEM((SPAN, PARTS * SUBS, LANES), F32)
    flat = pltpu.VMEM((PARTS, SPAN, LANES), F32)
    return pl.pallas_call(
        kernel,
        out_shape=jax.ShapeDtypeStruct((sources // 4, rows, depth), F32),
        in_specs=[pl.BlockSpec(memory_space=pltpu.HBM)] * len(arrays),
        out_specs=pl.BlockSpec(memory_space=pltpu.VMEM),
        scratch_shapes=[
            pltpu.VMEM(fields.shape, fields.dtype),
            pltpu.VMEM((rows, depth), F32),
            *small,
            pltpu.VMEM((depth, depth), BF16),
            pltpu.VMEM((depth, depth), BF16),
            pltpu.VMEM((SUBS * rows, SUBS * rows), BF16),
            pltpu.VMEM((4, HELD * SUBS, depth), BF16),
            pltpu.VMEM((HALO, depth), F32),
            pltpu.VMEM((HALO, depth), F32),
            flat, flat, flat, flat,
            tall, tall, tall, tall,
            pltpu.VMEM((3 * ITERS, PARTS * SUBS, LANES), F32),
            pltpu.VMEM((2, SPAN, SUBS, LANES), F32),
            pltpu.VMEM((2, SPAN, PARTS * SUBS, LANES), F32),
            pltpu.VMEM((sources, PARTS, rows, LANES), F32),
            pltpu.VMEM((3, PARTS, rows, LANES), F32),
            pltpu.VMEM((3, PARTS, rows, LANES), F32),
            pltpu.SemaphoreType.DMA((10,)),
            pltpu.SemaphoreType.DMA((2, 4)),
            pltpu.SemaphoreType.DMA((2, 4)),
            pltpu.SemaphoreType.DMA((2,)),
            pltpu.SemaphoreType.DMA((2,)),
            pltpu.SemaphoreType.DMA((2, 3)),
            pltpu.SemaphoreType.DMA((2, 3)),
        ],
        compiler_params=pltpu.CompilerParams(
            collective_id=0, has_side_effects=True, vmem_limit_bytes=63 * 1024 * 1024),
    )(*arrays)


def solution(mesh):
    placed = (P("wave", None, "tile", None), P("tile", None), P(), P(), P(), P(), P())
    return jax.shard_map(
        local, mesh=mesh, in_specs=placed, out_specs=P("wave", "tile", None), check_vma=False
    )
```

```python
import jax
import jax.numpy as jnp
from jax import lax
from jax.experimental import pallas as pl
from jax.experimental.pallas import tpu as pltpu
from jax.sharding import PartitionSpec as P

ITERS = 8
LOWER = 0.1
UPPER = 2.0
THETA = (UPPER + LOWER) / 2.0
DELTA = (UPPER - LOWER) / 2.0
SIGMA_ONE = THETA / DELTA
CURRENT = 2.0

TAU = [1.0, SIGMA_ONE]
for _ in range(ITERS):
    TAU.append(2.0 * SIGMA_ONE * TAU[-1] - TAU[-2])
OMEGA = 2.0 * (THETA - 1.0) / DELTA

LANES = 128
SUBS = 8
PARTS = 8
ROWS = 32
HALO = 8
HELD = ROWS + 2 * HALO
SPAN = 64
FIRST = 8
CORE = FIRST + HALO
LAST = FIRST + HELD
UNROLL = ((8, 6), (15, 3), (22, 2), (21, 2), (13, 3), (19, 2), (18, 2), (17, 2))
FIRST_TWINS = 11
MESH = pl.DeviceIdType.MESH
F32 = jnp.float32
BF16 = jnp.bfloat16


def chosen(index, table):
    value = jnp.float32(0.0)
    for position, entry in enumerate(table):
        value = jnp.where(index == position, jnp.float32(entry), value)
    return value


def slot_column(pair, half, wave_pos):
    middle = jnp.logical_or(pair == 1, pair == 2)
    ahead = jnp.where(pair == 0, 2, jnp.where(middle, 1 + 2 * half, 0))
    offset = jnp.where(middle, pair - 1, half)
    return 2 * lax.rem(wave_pos + ahead, 4) + offset


def thirds(values):
    high = values.astype(BF16)
    rest = values - high.astype(F32)
    middle = rest.astype(BF16)
    low = (rest - middle.astype(F32)).astype(BF16)
    return high, middle, low


def kernel(
    fields_in, sigma_in, wavenumbers_in, weights_in, counts_in, electrodes_in, pairs_in, out,
    fields, sigma, wavenumbers, weights, counts, electrodes, pairs,
    into, back, weave, stage, sig_n, sig_s, sig, diag, face_n, face_w,
    an, aw, root, close, vectors, src, w, acc, from_low, from_high,
    in_sem, h_send, h_recv, s_send, s_recv, r_send, r_recv,
):
    per_group = fields.shape[0]
    tile_count = lax.axis_size("tile")
    wave_count = lax.axis_size("wave")
    tile_pos = lax.axis_index("tile")
    wave_pos = lax.axis_index("wave")
    south = {"tile": lax.rem(tile_pos + 1, tile_count)}
    north = {"tile": lax.rem(tile_pos + tile_count - 1, tile_count)}
    above = {"wave": lax.rem(wave_pos + 1, wave_count)}
    below = {"wave": lax.rem(wave_pos + wave_count - 1, wave_count)}

    barrier = pltpu.get_barrier_semaphore()
    for other in (south, north, above, below):
        pl.semaphore_signal(barrier, inc=1, device_id=other, device_id_type=MESH)

    def remote(source, target, send, recv, device):
        return pltpu.make_async_remote_copy(
            src_ref=source, dst_ref=target, send_sem=send, recv_sem=recv,
            device_id=device, device_id_type=MESH,
        )

    sources = [(fields_in.at[k], fields.at[k]) for k in range(per_group)] + [
        (sigma_in, sigma), (wavenumbers_in, wavenumbers), (weights_in, weights),
        (counts_in, counts), (electrodes_in, electrodes), (pairs_in, pairs)]
    loads = [
        pltpu.make_async_copy(source, target, in_sem.at[place]) for place, (source, target) in enumerate(sources)]
    for load in loads:
        load.start()
    sig_south = remote(sigma_in.at[pl.ds(ROWS - HALO, HALO)], sig_n, s_send.at[0], s_recv.at[0], south)
    sig_north = remote(sigma_in.at[pl.ds(0, HALO)], sig_s, s_send.at[1], s_recv.at[1], north)

    lane = lax.broadcasted_iota(jnp.int32, (SUBS, LANES), 1)
    sub = lax.broadcasted_iota(jnp.int32, (SUBS, LANES), 0)
    first_lane = lane == 0
    last_lane = lane == LANES - 1
    zero = jnp.zeros((SUBS, LANES), F32)

    @pl.loop(0, PARTS)
    def _(block):
        wide = PARTS * LANES
        base = pl.multiple_of(block * LANES, LANES)
        row = lax.broadcasted_iota(jnp.int32, (LANES, wide), 0) + base
        column = lax.broadcasted_iota(jnp.int32, (LANES, wide), 1)
        into[pl.ds(base, LANES), :] = jnp.where(
            row == lax.rem(column, LANES) * PARTS + lax.div(column, LANES), 1.0, 0.0).astype(BF16)
        back[pl.ds(base, LANES), :] = jnp.where(
            column == lax.rem(row, LANES) * PARTS + lax.div(row, LANES), 1.0, 0.0).astype(BF16)

    row = lax.broadcasted_iota(jnp.int32, weave.shape, 0)
    column = lax.broadcasted_iota(jnp.int32, weave.shape, 1)
    weave[...] = jnp.where(
        column == lax.rem(row, SUBS) * ROWS + lax.div(row, SUBS), 1.0, 0.0).astype(BF16)

    for part in range(PARTS):
        rows8 = pl.ds(part * SUBS, SUBS)
        for row in range(LAST, SPAN):
            an[row, rows8, :] = zero
            aw[row, rows8, :] = zero
            src[0, row] = zero
            for buf in range(2):
                w[buf, row, rows8, :] = zero
        for edge in (0, LAST):
            sig[part, pl.ds(edge, FIRST), :] = zero + 1.0

    pl.semaphore_wait(barrier, 4)
    sig_south.start()
    sig_north.start()

    for load in loads:
        load.wait()
    def halo_copies(pair):
        return (
            remote(stage.at[pair, pl.ds(ROWS * SUBS, HALO * SUBS)], stage.at[pair, pl.ds(0, HALO * SUBS)],
                   h_send.at[0, pair], h_recv.at[0, pair], south),
            remote(stage.at[pair, pl.ds(HALO * SUBS, HALO * SUBS)],
                   stage.at[pair, pl.ds((HALO + ROWS) * SUBS, HALO * SUBS)],
                   h_send.at[1, pair], h_recv.at[1, pair], north),
        )

    @pl.loop(0, 2)
    def _(batch):
        woven = []
        for pair in (2 * batch, 2 * batch + 1):
            columns = [slot_column(pair, half, wave_pos) for half in range(2)]
            block = jnp.concatenate(
                [fields[k, columns[half]] for half in range(2) for k in range(per_group)], axis=0)
            woven.append(jnp.dot(weave[...], block, preferred_element_type=F32).astype(BF16))
        moved = jnp.dot(jnp.concatenate(woven, axis=0), into[...], preferred_element_type=F32).astype(BF16)
        for place, pair in enumerate((2 * batch, 2 * batch + 1)):
            stage[pair, pl.ds(HALO * SUBS, ROWS * SUBS), :] = moved[place * ROWS * SUBS:(place + 1) * ROWS * SUBS]
            for copy in halo_copies(pair):
                copy.start()

    def by_wavenumber(scalars):
        value = zero
        for k, scalar in enumerate(scalars):
            value = jnp.where(lax.rem(sub, per_group) == k, scalar, value)
        return value

    def everywhere(scalars):
        return jnp.concatenate([by_wavenumber(scalars)] * PARTS, axis=0)

    group = [wave_pos * per_group + k for k in range(per_group)]
    square = by_wavenumber([wavenumbers[g] * wavenumbers[g] for g in group])
    final = by_wavenumber([
        weights[g] * chosen(counts[g], [1.0 / tau for tau in TAU[: ITERS + 1]]) for g in group])
    for step in range(ITERS):
        live = [step - (ITERS - counts[g]) for g in group]
        vectors[3 * step] = everywhere([
            jnp.where(at < 0, F32(2.0), jnp.where(at == 0, F32(1.0 + 0.5 * OMEGA), F32(OMEGA))) for at in live])
        vectors[3 * step + 1] = everywhere([
            jnp.where(at < 0, F32(0.0), jnp.where(at == 0, F32(0.5), F32(1.0))) for at in live])
        vectors[3 * step + 2] = everywhere([chosen(at, [0.5] + TAU[1:ITERS]) for at in live])

    sig_south.wait_recv()
    sig_north.wait_recv()
    whole = jnp.concatenate([sig_n[...], sigma[...], sig_s[...]], axis=0)
    moved = jnp.dot(jnp.concatenate(thirds(whole), axis=0), into[...], preferred_element_type=F32)
    moved = (moved[:HELD] + moved[HELD:2 * HELD]) + moved[2 * HELD:]
    for part in range(PARTS):
        sig[part, pl.ds(FIRST, HELD), :] = moved[:, part * LANES:(part + 1) * LANES]

    @pl.loop(1, LAST // SUBS)
    def _(row_tile):
        row = pl.multiple_of(row_tile * SUBS, SUBS)
        place = tile_pos * ROWS + row - CORE + sub
        last_row = tile_count * ROWS
        centre = [sig[part, pl.ds(row, SUBS), :] for part in range(PARTS)]
        for part in range(PARTS):
            mid = centre[part]
            up = jnp.where(place == 0, 0.0, sig[part, pl.ds(row - 1, SUBS), :])
            down = jnp.where(place == last_row - 1, 0.0, sig[part, pl.ds(row + 1, SUBS), :])
            if part == 0:
                left = jnp.where(first_lane, 0.0, pltpu.roll(centre[-1], 1, 1))
            else:
                left = centre[part - 1]
            if part == PARTS - 1:
                right = jnp.where(last_lane, 0.0, pltpu.roll(centre[0], LANES - 1, 1))
            else:
                right = centre[part + 1]
            faces = [0.5 * (mid + near) for near in (up, down, left, right)]
            diag[part, pl.ds(row, SUBS), :] = (faces[0] + faces[1]) + (faces[2] + faces[3])
            outside = jnp.logical_or(place == 0, place == last_row)
            face_n[part, pl.ds(row, SUBS), :] = jnp.where(outside, 0.0, (2.0 / DELTA) * faces[0])
            west = (2.0 / DELTA) * faces[2]
            if part == 0:
                west = jnp.where(first_lane, 0.0, west)
            face_w[part, pl.ds(row, SUBS), :] = west

    def couplings(row, above_row):
        def spread(ref, part):
            return jnp.broadcast_to(ref[part, pl.ds(row, 1), :], (SUBS, LANES))

        here = []
        for part in range(PARTS):
            rows8 = pl.ds(part * SUBS, SUBS)
            value = spread(diag, part) + square * spread(sig, part)
            guess = lax.rsqrt(value)
            root[row, rows8, :] = value * guess
            close[row, rows8, :] = final * guess
            an[row, rows8, :] = spread(face_n, part) * (guess * above_row[part])
            here.append(guess)
        src[1, row] = here[0]
        for part in range(PARTS):
            beside = here[part - 1] if part else pltpu.roll(here[-1], 1, 1)
            aw[row, pl.ds(part * SUBS, SUBS), :] = spread(face_w, part) * (here[part] * beside)
        return tuple(here)

    def four_rows(block, above_row):
        for place in range(4):
            above_row = couplings(FIRST + 4 * block + place, above_row)
        return above_row

    lax.fori_loop(0, HELD // 4, four_rows, (zero,) * PARTS)

    def sweep(step, pair, spots):
        now, later = step % 2, (step + 1) % 2
        charge = vectors[3 * step + 2, pl.ds(0, SUBS), :]
        start = FIRST + step + 1
        unroll, blocks = UNROLL[step]
        parts = [pl.ds(part * SUBS, SUBS) for part in range(PARTS)]

        def one(row, carry, u):
            old, sums = carry
            edge = pltpu.roll(u[-1], 1, 1)
            held, flow_first = [], None
            if step == 0:
                spot = jnp.where(row - 1 == spots[0], CURRENT, 0.0) - jnp.where(row - 1 == spots[1], CURRENT, 0.0)
                source = jnp.where(first_lane, (2.0 / DELTA) * spot * src[1, row - 1], 0.0)
                src[0, row - 1] = source
            else:
                source = src[0, row - 1]
            for part, at in enumerate(parts):
                here = u[part]
                north_c = an[row, at, :]
                side_gain, centre_gain = vectors[3 * step + 1, at, :], vectors[3 * step, at, :]
                if step == 0:
                    value = side_gain * (sums[part] + north_c * here) + (centre_gain - 1.0) * old[part]
                else:
                    value = side_gain * (sums[part] + north_c * here) + (
                        centre_gain * old[part] - w[later, row - 1, at, :])
                if part == 0:
                    value = value + charge * source
                w[later, row - 1, at, :] = value
                west_c = aw[row, at, :]
                flow = west_c * here
                if part == 0:
                    flow_first = pltpu.roll(flow, LANES - 1, 1)
                else:
                    held[-1] = held[-1] + flow
                held.append(north_c * old[part] + west_c * (u[part - 1] if part else edge))
            held[-1] = held[-1] + flow_first
            return tuple(u), tuple(held)

        def given(twin):
            both = [[], []]
            for part, at in enumerate(parts):
                values = stage[pair, pl.ds(twin * 2 * SUBS, 2 * SUBS), pl.ds(part * LANES, LANES)].astype(F32)
                for place in range(2):
                    row = FIRST + 2 * twin + place
                    value = values[place * SUBS:(place + 1) * SUBS] * root[row, at, :]
                    w[0, row, at, :] = value
                    both[place].append(value)
            return both

        def two(twin, carry):
            row = FIRST + 2 * twin
            for place, u in enumerate(given(twin)):
                carry = one(row + place, carry, u)
            return carry

        if step == 0:
            opening, second = given(0)
            carry = one(FIRST + 1, (tuple(opening), (zero,) * PARTS), second)
            carry = two(1, carry)

            def several(block, carry):
                for place in range(FIRST_TWINS):
                    carry = two(2 + FIRST_TWINS * block + place, carry)
                return carry

            lax.fori_loop(0, (HELD // 2 - 2) // FIRST_TWINS, several, carry)
        else:

            def body(block, carry):
                for place in range(unroll):
                    row = start + unroll * block + place
                    carry = one(row, carry, [w[now, row, at, :] for at in parts])
                return carry

            opening = tuple(w[now, start - 1, at, :] for at in parts)
            lax.fori_loop(0, blocks, body, (opening, (zero,) * PARTS))

    def rs_copies(pair):
        slot = 2 * pair
        return (
            remote(acc.at[slot], from_low.at[pair], r_send.at[0, pair], r_recv.at[0, pair], above),
            remote(acc.at[slot + 1], from_high.at[pair], r_send.at[1, pair], r_recv.at[1, pair], below),
        )

    @pl.loop(0, 4)
    def _(pair):
        columns = [slot_column(pair, half, wave_pos) for half in range(2)]
        spots = []
        for end in range(2):
            low, high = [electrodes[pairs[end, column]] for column in columns]
            spots.append(jnp.where(sub < per_group, low, high) - tile_pos * ROWS + CORE)
        for copy in halo_copies(pair):
            copy.wait_recv()

        for step in range(ITERS):
            sweep(step, pair, spots)

        @pl.loop(0, ROWS // 8)
        def _(block):
            for row in [8 * block + place for place in range(8)]:
                for part in range(PARTS):
                    rows8 = pl.ds(part * SUBS, SUBS)
                    value = close[CORE + row, rows8, :] * w[ITERS % 2, CORE + row, rows8, :]
                    value = value + pltpu.roll(value, SUBS - 2, 0)
                    value = value + pltpu.roll(value, SUBS - 1, 0)
                    for half in range(2):
                        acc[2 * pair + half, part, pl.ds(row, 1), :] = value[half * per_group:half * per_group + 1]

        @pl.when(pair == 1)
        def _():
            rs_copies(0)[0].wait_recv()
            acc[2] += from_low[0]

        @pl.when(pair == 2)
        def _():
            rs_copies(0)[1].wait_recv()
            acc[5] += from_high[0]

        @pl.when(pair < 3)
        def _():
            for copy in rs_copies(pair):
                copy.start()

    for pair in (1, 2):
        for copy in rs_copies(pair):
            copy.wait_recv()
    total = jnp.concatenate([
        jnp.concatenate([acc[6 + half, part] + (from_low[1 + half, part] + from_high[1 + half, part])
                         for part in range(PARTS)], axis=1)
        for half in range(2)], axis=0)
    moved = jnp.dot(jnp.concatenate(thirds(total), axis=0), back[...], preferred_element_type=F32)
    for half in range(2):
        cut = half * ROWS
        out[half] = (moved[cut:cut + ROWS] + moved[2 * ROWS + cut:3 * ROWS + cut]) + moved[
            4 * ROWS + cut:5 * ROWS + cut]

    for pair in range(3):
        for copy in rs_copies(pair):
            copy.wait_send()
    for pair in range(4):
        for copy in halo_copies(pair):
            copy.wait_send()
    sig_south.wait_send()
    sig_north.wait_send()


def local(*arrays):
    arrays = (*arrays[:-1], arrays[-1].T)
    fields = arrays[0]
    per_group, sources, rows, depth = fields.shape
    small = [pltpu.SMEM(a.shape, a.dtype) for a in arrays[2:]]
    tall = pltpu.VMEM((SPAN, PARTS * SUBS, LANES), F32)
    flat = pltpu.VMEM((PARTS, SPAN, LANES), F32)
    return pl.pallas_call(
        kernel,
        out_shape=jax.ShapeDtypeStruct((sources // 4, rows, depth), F32),
        in_specs=[pl.BlockSpec(memory_space=pltpu.HBM)] * len(arrays),
        out_specs=pl.BlockSpec(memory_space=pltpu.VMEM),
        scratch_shapes=[
            pltpu.VMEM(fields.shape, fields.dtype),
            pltpu.VMEM((rows, depth), F32),
            *small,
            pltpu.VMEM((depth, depth), BF16),
            pltpu.VMEM((depth, depth), BF16),
            pltpu.VMEM((SUBS * rows, SUBS * rows), BF16),
            pltpu.VMEM((4, HELD * SUBS, depth), BF16),
            pltpu.VMEM((HALO, depth), F32),
            pltpu.VMEM((HALO, depth), F32),
            flat, flat, flat, flat,
            tall, tall, tall, tall,
            pltpu.VMEM((3 * ITERS, PARTS * SUBS, LANES), F32),
            pltpu.VMEM((2, SPAN, SUBS, LANES), F32),
            pltpu.VMEM((2, SPAN, PARTS * SUBS, LANES), F32),
            pltpu.VMEM((sources, PARTS, rows, LANES), F32),
            pltpu.VMEM((3, PARTS, rows, LANES), F32),
            pltpu.VMEM((3, PARTS, rows, LANES), F32),
            pltpu.SemaphoreType.DMA((10,)),
            pltpu.SemaphoreType.DMA((2, 4)),
            pltpu.SemaphoreType.DMA((2, 4)),
            pltpu.SemaphoreType.DMA((2,)),
            pltpu.SemaphoreType.DMA((2,)),
            pltpu.SemaphoreType.DMA((2, 3)),
            pltpu.SemaphoreType.DMA((2, 3)),
        ],
        compiler_params=pltpu.CompilerParams(
            collective_id=0, has_side_effects=True, vmem_limit_bytes=63 * 1024 * 1024),
    )(*arrays)


def solution(mesh):
    placed = (P("wave", None, "tile", None), P("tile", None), P(), P(), P(), P(), P())
    return jax.shard_map(
        local, mesh=mesh, in_specs=placed, out_specs=P("wave", "tile", None), check_vma=False
    )
```

```python
import jax
import jax.numpy as jnp
from jax import lax
from jax.experimental import pallas as pl
from jax.experimental.pallas import tpu as pltpu
from jax.sharding import PartitionSpec as P

ITERS = 8
LOWER = 0.1
UPPER = 2.0
THETA = (UPPER + LOWER) / 2.0
DELTA = (UPPER - LOWER) / 2.0
SIGMA_ONE = THETA / DELTA
CURRENT = 2.0

TAU = [1.0, SIGMA_ONE]
for _ in range(ITERS):
    TAU.append(2.0 * SIGMA_ONE * TAU[-1] - TAU[-2])
OMEGA = 2.0 * (THETA - 1.0) / DELTA

LANES = 128
SUBS = 8
PARTS = 8
ROWS = 32
HALO = 8
HELD = ROWS + 2 * HALO
SPAN = 64
FIRST = 8
CORE = FIRST + HALO
LAST = FIRST + HELD
UNROLL = ((8, 6), (15, 3), (22, 2), (21, 2), (13, 3), (19, 2), (18, 2), (17, 2))
FIRST_TWINS = 11
MESH = pl.DeviceIdType.MESH
F32 = jnp.float32
BF16 = jnp.bfloat16


def chosen(index, table):
    value = jnp.float32(0.0)
    for position, entry in enumerate(table):
        value = jnp.where(index == position, jnp.float32(entry), value)
    return value


def slot_column(pair, half, wave_pos):
    middle = jnp.logical_or(pair == 1, pair == 2)
    ahead = jnp.where(pair == 0, 2, jnp.where(middle, 1 + 2 * half, 0))
    offset = jnp.where(middle, pair - 1, half)
    return 2 * lax.rem(wave_pos + ahead, 4) + offset


def thirds(values):
    high = values.astype(BF16)
    rest = values - high.astype(F32)
    middle = rest.astype(BF16)
    low = (rest - middle.astype(F32)).astype(BF16)
    return high, middle, low


def kernel(
    fields_in, sigma_in, wavenumbers_in, weights_in, counts_in, electrodes_in, pairs_in, out,
    fields, sigma, wavenumbers, weights, counts, electrodes, pairs,
    into, back, weave, stage, sig_n, sig_s, sig, diag, face_n, face_w,
    an, aw, root, close, vectors, src, w, acc, from_low, from_high,
    in_sem, h_send, h_recv, s_send, s_recv, r_send, r_recv,
):
    per_group = fields.shape[0]
    tile_count = lax.axis_size("tile")
    wave_count = lax.axis_size("wave")
    tile_pos = lax.axis_index("tile")
    wave_pos = lax.axis_index("wave")
    south = {"tile": lax.rem(tile_pos + 1, tile_count)}
    north = {"tile": lax.rem(tile_pos + tile_count - 1, tile_count)}
    above = {"wave": lax.rem(wave_pos + 1, wave_count)}
    below = {"wave": lax.rem(wave_pos + wave_count - 1, wave_count)}

    barrier = pltpu.get_barrier_semaphore()
    for other in (south, north, above, below):
        pl.semaphore_signal(barrier, inc=1, device_id=other, device_id_type=MESH)

    def remote(source, target, send, recv, device):
        return pltpu.make_async_remote_copy(
            src_ref=source, dst_ref=target, send_sem=send, recv_sem=recv,
            device_id=device, device_id_type=MESH,
        )

    sources = [(fields_in.at[k], fields.at[k]) for k in range(per_group)] + [
        (sigma_in, sigma), (wavenumbers_in, wavenumbers), (weights_in, weights),
        (counts_in, counts), (electrodes_in, electrodes), (pairs_in, pairs)]
    loads = [
        pltpu.make_async_copy(source, target, in_sem.at[place]) for place, (source, target) in enumerate(sources)]
    for load in loads:
        load.start()
    sig_south = remote(sigma_in.at[pl.ds(ROWS - HALO, HALO)], sig_n, s_send.at[0], s_recv.at[0], south)
    sig_north = remote(sigma_in.at[pl.ds(0, HALO)], sig_s, s_send.at[1], s_recv.at[1], north)

    lane = lax.broadcasted_iota(jnp.int32, (SUBS, LANES), 1)
    sub = lax.broadcasted_iota(jnp.int32, (SUBS, LANES), 0)
    first_lane = lane == 0
    last_lane = lane == LANES - 1
    zero = jnp.zeros((SUBS, LANES), F32)

    @pl.loop(0, PARTS)
    def _(block):
        wide = PARTS * LANES
        base = pl.multiple_of(block * LANES, LANES)
        row = lax.broadcasted_iota(jnp.int32, (LANES, wide), 0) + base
        column = lax.broadcasted_iota(jnp.int32, (LANES, wide), 1)
        into[pl.ds(base, LANES), :] = jnp.where(
            row == lax.rem(column, LANES) * PARTS + lax.div(column, LANES), 1.0, 0.0).astype(BF16)
        back[pl.ds(base, LANES), :] = jnp.where(
            column == lax.rem(row, LANES) * PARTS + lax.div(row, LANES), 1.0, 0.0).astype(BF16)

    row = lax.broadcasted_iota(jnp.int32, weave.shape, 0)
    column = lax.broadcasted_iota(jnp.int32, weave.shape, 1)
    weave[...] = jnp.where(
        column == lax.rem(row, SUBS) * ROWS + lax.div(row, SUBS), 1.0, 0.0).astype(BF16)

    for part in range(PARTS):
        rows8 = pl.ds(part * SUBS, SUBS)
        for row in range(LAST, SPAN):
            an[row, rows8, :] = zero
            aw[row, rows8, :] = zero
            src[0, row] = zero
            for buf in range(2):
                w[buf, row, rows8, :] = zero
        for edge in (0, LAST):
            sig[part, pl.ds(edge, FIRST), :] = zero + 1.0

    pl.semaphore_wait(barrier, 4)
    sig_south.start()
    sig_north.start()

    for load in loads:
        load.wait()
    def halo_copies(pair):
        return (
            remote(stage.at[pair, pl.ds(ROWS * SUBS, HALO * SUBS)], stage.at[pair, pl.ds(0, HALO * SUBS)],
                   h_send.at[0, pair], h_recv.at[0, pair], south),
            remote(stage.at[pair, pl.ds(HALO * SUBS, HALO * SUBS)],
                   stage.at[pair, pl.ds((HALO + ROWS) * SUBS, HALO * SUBS)],
                   h_send.at[1, pair], h_recv.at[1, pair], north),
        )

    def gather(batch, extra):
        woven = []
        for pair in (2 * batch, 2 * batch + 1):
            columns = [slot_column(pair, half, wave_pos) for half in range(2)]
            block = jnp.concatenate(
                [fields[k, columns[half]] for half in range(2) for k in range(per_group)], axis=0)
            woven.append(jnp.dot(weave[...], block, preferred_element_type=F32).astype(BF16))
        moved = jnp.dot(jnp.concatenate(woven + extra, axis=0), into[...], preferred_element_type=F32)
        for place, pair in enumerate((2 * batch, 2 * batch + 1)):
            stage[pair, pl.ds(HALO * SUBS, ROWS * SUBS), :] = moved[
                place * ROWS * SUBS:(place + 1) * ROWS * SUBS].astype(BF16)
            for copy in halo_copies(pair):
                copy.start()
        return moved[2 * ROWS * SUBS:]

    gather(0, [])

    def by_wavenumber(scalars):
        value = zero
        for k, scalar in enumerate(scalars):
            value = jnp.where(lax.rem(sub, per_group) == k, scalar, value)
        return value

    def everywhere(scalars):
        return jnp.concatenate([by_wavenumber(scalars)] * PARTS, axis=0)

    group = [wave_pos * per_group + k for k in range(per_group)]
    square = by_wavenumber([wavenumbers[g] * wavenumbers[g] for g in group])
    final = by_wavenumber([
        weights[g] * chosen(counts[g], [1.0 / tau for tau in TAU[: ITERS + 1]]) for g in group])
    for step in range(ITERS):
        live = [step - (ITERS - counts[g]) for g in group]
        vectors[3 * step] = everywhere([
            jnp.where(at < 0, F32(2.0), jnp.where(at == 0, F32(1.0 + 0.5 * OMEGA), F32(OMEGA))) for at in live])
        vectors[3 * step + 1] = everywhere([
            jnp.where(at < 0, F32(0.0), jnp.where(at == 0, F32(0.5), F32(1.0))) for at in live])
        vectors[3 * step + 2] = everywhere([chosen(at, [0.5] + TAU[1:ITERS]) for at in live])

    sig_south.wait_recv()
    sig_north.wait_recv()
    whole = jnp.concatenate([sig_n[...], sigma[...], sig_s[...]], axis=0)
    moved = gather(1, list(thirds(whole)))
    moved = (moved[:HELD] + moved[HELD:2 * HELD]) + moved[2 * HELD:]
    for part in range(PARTS):
        sig[part, pl.ds(FIRST, HELD), :] = moved[:, part * LANES:(part + 1) * LANES]

    @pl.loop(1, LAST // SUBS)
    def _(row_tile):
        row = pl.multiple_of(row_tile * SUBS, SUBS)
        place = tile_pos * ROWS + row - CORE + sub
        last_row = tile_count * ROWS
        centre = [sig[part, pl.ds(row, SUBS), :] for part in range(PARTS)]
        for part in range(PARTS):
            mid = centre[part]
            up = jnp.where(place == 0, 0.0, sig[part, pl.ds(row - 1, SUBS), :])
            down = jnp.where(place == last_row - 1, 0.0, sig[part, pl.ds(row + 1, SUBS), :])
            if part == 0:
                left = jnp.where(first_lane, 0.0, pltpu.roll(centre[-1], 1, 1))
            else:
                left = centre[part - 1]
            if part == PARTS - 1:
                right = jnp.where(last_lane, 0.0, pltpu.roll(centre[0], LANES - 1, 1))
            else:
                right = centre[part + 1]
            faces = [0.5 * (mid + near) for near in (up, down, left, right)]
            diag[part, pl.ds(row, SUBS), :] = (faces[0] + faces[1]) + (faces[2] + faces[3])
            outside = jnp.logical_or(place == 0, place == last_row)
            face_n[part, pl.ds(row, SUBS), :] = jnp.where(outside, 0.0, (2.0 / DELTA) * faces[0])
            west = (2.0 / DELTA) * faces[2]
            if part == 0:
                west = jnp.where(first_lane, 0.0, west)
            face_w[part, pl.ds(row, SUBS), :] = west

    def couplings(row, above_row):
        def spread(ref, part):
            return jnp.broadcast_to(ref[part, pl.ds(row, 1), :], (SUBS, LANES))

        here = []
        for part in range(PARTS):
            rows8 = pl.ds(part * SUBS, SUBS)
            value = spread(diag, part) + square * spread(sig, part)
            guess = lax.rsqrt(value)
            root[row, rows8, :] = value * guess
            close[row, rows8, :] = final * guess
            an[row, rows8, :] = spread(face_n, part) * (guess * above_row[part])
            here.append(guess)
        src[1, row] = here[0]
        for part in range(PARTS):
            beside = here[part - 1] if part else pltpu.roll(here[-1], 1, 1)
            aw[row, pl.ds(part * SUBS, SUBS), :] = spread(face_w, part) * (here[part] * beside)
        return tuple(here)

    def four_rows(block, above_row):
        for place in range(4):
            above_row = couplings(FIRST + 4 * block + place, above_row)
        return above_row

    lax.fori_loop(0, HELD // 4, four_rows, (zero,) * PARTS)

    def sweep(step, pair, spots):
        now, later = step % 2, (step + 1) % 2
        charge = vectors[3 * step + 2, pl.ds(0, SUBS), :]
        start = FIRST + step + 1
        unroll, blocks = UNROLL[step]
        parts = [pl.ds(part * SUBS, SUBS) for part in range(PARTS)]

        def one(row, carry, u):
            old, sums = carry
            edge = pltpu.roll(u[-1], 1, 1)
            held, flow_first = [], None
            if step == 0:
                spot = jnp.where(row - 1 == spots[0], CURRENT, 0.0) - jnp.where(row - 1 == spots[1], CURRENT, 0.0)
                source = jnp.where(first_lane, (2.0 / DELTA) * spot * src[1, row - 1], 0.0)
                src[0, row - 1] = source
            else:
                source = src[0, row - 1]
            for part, at in enumerate(parts):
                here = u[part]
                north_c = an[row, at, :]
                side_gain, centre_gain = vectors[3 * step + 1, at, :], vectors[3 * step, at, :]
                if step == 0:
                    value = side_gain * (sums[part] + north_c * here) + (centre_gain - 1.0) * old[part]
                else:
                    value = side_gain * (sums[part] + north_c * here) + (
                        centre_gain * old[part] - w[later, row - 1, at, :])
                if part == 0:
                    value = value + charge * source
                w[later, row - 1, at, :] = value
                west_c = aw[row, at, :]
                flow = west_c * here
                if part == 0:
                    flow_first = pltpu.roll(flow, LANES - 1, 1)
                else:
                    held[-1] = held[-1] + flow
                held.append(north_c * old[part] + west_c * (u[part - 1] if part else edge))
            held[-1] = held[-1] + flow_first
            return tuple(u), tuple(held)

        def given(twin):
            both = [[], []]
            for part, at in enumerate(parts):
                values = stage[pair, pl.ds(twin * 2 * SUBS, 2 * SUBS), pl.ds(part * LANES, LANES)].astype(F32)
                for place in range(2):
                    row = FIRST + 2 * twin + place
                    value = values[place * SUBS:(place + 1) * SUBS] * root[row, at, :]
                    w[0, row, at, :] = value
                    both[place].append(value)
            return both

        def two(twin, carry):
            row = FIRST + 2 * twin
            for place, u in enumerate(given(twin)):
                carry = one(row + place, carry, u)
            return carry

        if step == 0:
            opening, second = given(0)
            carry = one(FIRST + 1, (tuple(opening), (zero,) * PARTS), second)
            carry = two(1, carry)

            def several(block, carry):
                for place in range(FIRST_TWINS):
                    carry = two(2 + FIRST_TWINS * block + place, carry)
                return carry

            lax.fori_loop(0, (HELD // 2 - 2) // FIRST_TWINS, several, carry)
        else:

            def body(block, carry):
                for place in range(unroll):
                    row = start + unroll * block + place
                    carry = one(row, carry, [w[now, row, at, :] for at in parts])
                return carry

            opening = tuple(w[now, start - 1, at, :] for at in parts)
            lax.fori_loop(0, blocks, body, (opening, (zero,) * PARTS))

    def rs_copies(pair):
        slot = 2 * pair
        return (
            remote(acc.at[slot], from_low.at[pair], r_send.at[0, pair], r_recv.at[0, pair], above),
            remote(acc.at[slot + 1], from_high.at[pair], r_send.at[1, pair], r_recv.at[1, pair], below),
        )

    @pl.loop(0, 4)
    def _(pair):
        columns = [slot_column(pair, half, wave_pos) for half in range(2)]
        spots = []
        for end in range(2):
            low, high = [electrodes[pairs[end, column]] for column in columns]
            spots.append(jnp.where(sub < per_group, low, high) - tile_pos * ROWS + CORE)
        for copy in halo_copies(pair):
            copy.wait_recv()

        for step in range(ITERS):
            sweep(step, pair, spots)

        @pl.loop(0, ROWS // 8)
        def _(block):
            for row in [8 * block + place for place in range(8)]:
                for part in range(PARTS):
                    rows8 = pl.ds(part * SUBS, SUBS)
                    value = close[CORE + row, rows8, :] * w[ITERS % 2, CORE + row, rows8, :]
                    value = value + pltpu.roll(value, SUBS - 2, 0)
                    value = value + pltpu.roll(value, SUBS - 1, 0)
                    for half in range(2):
                        acc[2 * pair + half, part, pl.ds(row, 1), :] = value[half * per_group:half * per_group + 1]

        @pl.when(pair == 1)
        def _():
            rs_copies(0)[0].wait_recv()
            acc[2] += from_low[0]

        @pl.when(pair == 2)
        def _():
            rs_copies(0)[1].wait_recv()
            acc[5] += from_high[0]

        @pl.when(pair < 3)
        def _():
            for copy in rs_copies(pair):
                copy.start()

    for pair in (1, 2):
        for copy in rs_copies(pair):
            copy.wait_recv()
    total = jnp.concatenate([
        jnp.concatenate([acc[6 + half, part] + (from_low[1 + half, part] + from_high[1 + half, part])
                         for part in range(PARTS)], axis=1)
        for half in range(2)], axis=0)
    moved = jnp.dot(jnp.concatenate(thirds(total), axis=0), back[...], preferred_element_type=F32)
    for half in range(2):
        cut = half * ROWS
        out[half] = (moved[cut:cut + ROWS] + moved[2 * ROWS + cut:3 * ROWS + cut]) + moved[
            4 * ROWS + cut:5 * ROWS + cut]

    for pair in range(3):
        for copy in rs_copies(pair):
            copy.wait_send()
    for pair in range(4):
        for copy in halo_copies(pair):
            copy.wait_send()
    sig_south.wait_send()
    sig_north.wait_send()


def local(*arrays):
    arrays = (*arrays[:-1], arrays[-1].T)
    fields = arrays[0]
    per_group, sources, rows, depth = fields.shape
    small = [pltpu.SMEM(a.shape, a.dtype) for a in arrays[2:]]
    tall = pltpu.VMEM((SPAN, PARTS * SUBS, LANES), F32)
    flat = pltpu.VMEM((PARTS, SPAN, LANES), F32)
    return pl.pallas_call(
        kernel,
        out_shape=jax.ShapeDtypeStruct((sources // 4, rows, depth), F32),
        in_specs=[pl.BlockSpec(memory_space=pltpu.HBM)] * len(arrays),
        out_specs=pl.BlockSpec(memory_space=pltpu.VMEM),
        scratch_shapes=[
            pltpu.VMEM(fields.shape, fields.dtype),
            pltpu.VMEM((rows, depth), F32),
            *small,
            pltpu.VMEM((depth, depth), BF16),
            pltpu.VMEM((depth, depth), BF16),
            pltpu.VMEM((SUBS * rows, SUBS * rows), BF16),
            pltpu.VMEM((4, HELD * SUBS, depth), BF16),
            pltpu.VMEM((HALO, depth), F32),
            pltpu.VMEM((HALO, depth), F32),
            flat, flat, flat, flat,
            tall, tall, tall, tall,
            pltpu.VMEM((3 * ITERS, PARTS * SUBS, LANES), F32),
            pltpu.VMEM((2, SPAN, SUBS, LANES), F32),
            pltpu.VMEM((2, SPAN, PARTS * SUBS, LANES), F32),
            pltpu.VMEM((sources, PARTS, rows, LANES), F32),
            pltpu.VMEM((3, PARTS, rows, LANES), F32),
            pltpu.VMEM((3, PARTS, rows, LANES), F32),
            pltpu.SemaphoreType.DMA((10,)),
            pltpu.SemaphoreType.DMA((2, 4)),
            pltpu.SemaphoreType.DMA((2, 4)),
            pltpu.SemaphoreType.DMA((2,)),
            pltpu.SemaphoreType.DMA((2,)),
            pltpu.SemaphoreType.DMA((2, 3)),
            pltpu.SemaphoreType.DMA((2, 3)),
        ],
        compiler_params=pltpu.CompilerParams(
            collective_id=0, has_side_effects=True, vmem_limit_bytes=63 * 1024 * 1024),
    )(*arrays)


def solution(mesh):
    placed = (P("wave", None, "tile", None), P("tile", None), P(), P(), P(), P(), P())
    return jax.shard_map(
        local, mesh=mesh, in_specs=placed, out_specs=P("wave", "tile", None), check_vma=False
    )
```
